256 devices in a mesh: dp: 16 (over z, core), tensor: 16 (over x, y).
Axes of the slice: x: 4, y: 4, z: 8, core: 2. Of those that a mesh axis runs over, the one named last changes fastest.
Arguments:
- hidden: bfloat16 [16384, 28672], P('dp', 'tensor'), may hold values from -6 to 6
- output_gradient: bfloat16 [16384, 8192], P('dp', 'tensor'), may hold values from -1.5 to 1.5
- block_adapter_index: int32 [128], P('dp'), may hold values from 0 to 511, as said below
- adapter_down_factors: bfloat16 [512, 16, 28672], P('dp', None, 'tensor'), may hold values from -0.03125 to 0.03125
- adapter_up_factors: bfloat16 [512, 16, 8192], P('dp', None, 'tensor'), may hold values from -0.0625 to 0.0625
Outputs:
- grad_hidden: bfloat16 [16384, 28672], P('dp', 'tensor')
- grad_a: bfloat16 [512, 16, 28672], P('dp', None, 'tensor')
- grad_b: bfloat16 [512, 16, 8192], P('dp', None, 'tensor')
The draws below stay inside these ranges and needn't reach their ends.
Inputs may be any that keep to these rules, and one draw needn't show every extreme that they name: `block_adapter_index`: adapter a belongs to owner a // 32. Among the 8 blocks of one index of dp at most 2 take adapters of one owner, and on every index some owner is taken by exactly 2 blocks.
All inputs are finite; a program needn't handle non-finite values.
Results may differ from the reference program's by a relative error of at most 0.0053.
Values may be sent and summed in bfloat16 or wider, within the bound.
A program may use at most 64 MiB of HBM per device.

```python
import jax
import jax.numpy as jnp
from jax import lax

MODEL_WIDTH = 8192
HIDDEN_WIDTH = 28672
ADAPTER_RANK = 16
BLOCK = 128
BLK_DEV = 8
ADP_OWN = 32
BLOCKS = 128
TOKENS = 16384
ADAPTER_TOTAL = 512


def draw_block_adapter_index(key, part):
    key = jax.random.fold_in(key, 11)
    owner_count = BLOCKS // BLK_DEV

    def one_device(dev_key):
        key_perm, key_order, key_local = jax.random.split(dev_key, 3)
        perm = jax.random.permutation(key_perm, owner_count)
        position = jnp.arange(BLK_DEV, dtype=jnp.int32)
        owners = perm[jnp.maximum(position - 1, 0)]
        order = jax.random.permutation(key_order, BLK_DEV)
        owners = owners[order]
        local_draws = jax.random.randint(key_local, (3, BLK_DEV), 0, ADP_OWN)
        local_ids = jnp.min(local_draws, axis=0)
        return (owners * ADP_OWN + local_ids).astype(jnp.int32)
    dev_keys = jax.random.split(key, owner_count)
    return jax.vmap(one_device)(dev_keys).reshape(-1)


def steps_of(own_key, extent, shards, smallest, top_value):
    def one(dim, shards_of):
        steps = jax.random.uniform(jax.random.fold_in(jax.random.fold_in(own_key, 6), dim), (shards_of,), jnp.float32, smallest / len(shards), top_value / len(shards))
        return jnp.repeat(jnp.exp(steps), extent[dim] // shards_of).reshape((-1,) + (1,) * (len(extent) - dim - 1))

    loudness = one(*shards[0])
    for cut in shards[1:]:
        loudness = loudness * one(*cut)
    return loudness


def scatter_about(rng, shape, spread, most, pieces=(), kind=jnp.bfloat16):
    drawn = spread * jax.random.normal(rng, shape, jnp.float32)
    if pieces:
        drawn = drawn * steps_of(rng, shape, pieces, -0.22, 0.18)
    return jnp.clip(drawn, -most, most).astype(kind)


def setup_inputs(seed: int = 0) -> dict:
    seeds = jax.random.split(jax.random.key(seed), 6)
    return {
        "hidden": scatter_about(seeds[0], (TOKENS, HIDDEN_WIDTH), 1.0, 6.0, ((0, 16), (1, 16))),
        "output_gradient": scatter_about(seeds[1], (TOKENS, MODEL_WIDTH), 0.25, 1.5, ((0, 16), (1, 16))),
        "block_adapter_index": draw_block_adapter_index(jax.random.fold_in(seeds[5], 71), 0),
        "adapter_down_factors": scatter_about(seeds[3], (ADAPTER_TOTAL, ADAPTER_RANK, HIDDEN_WIDTH), HIDDEN_WIDTH ** -0.5, 0.03125, ((0, 16), (2, 16))),
        "adapter_up_factors": scatter_about(seeds[4], (ADAPTER_TOTAL, ADAPTER_RANK, MODEL_WIDTH), MODEL_WIDTH ** -0.5, 0.0625, ((0, 16), (2, 16))),
    }


adapter_scale = 2.0


def reference(hidden, output_gradient, block_adapter_index, adapter_down_factors, adapter_up_factors):
    hid_blocks = hidden.reshape(BLOCKS, BLOCK, HIDDEN_WIDTH)
    out_blocks = output_gradient.reshape(BLOCKS, BLOCK, MODEL_WIDTH)

    def one_block(items):
        hidden_rows, output_rows, adapter_index = items
        down_factor = adapter_down_factors[adapter_index]
        up_factor = adapter_up_factors[adapter_index]
        proj = jnp.dot(hidden_rows, down_factor.T, preferred_element_type=jnp.float32)
        back = jnp.dot(output_rows, up_factor.T, preferred_element_type=jnp.float32)
        projected_up = proj.astype(jnp.bfloat16)
        backward_up = back.astype(jnp.bfloat16)
        gradient_rows = (adapter_scale * jnp.dot(backward_up, down_factor, preferred_element_type=jnp.float32)).astype(jnp.bfloat16)
        block_down_gradient = (adapter_scale * jnp.dot(backward_up.T, hidden_rows, preferred_element_type=jnp.float32)).astype(jnp.bfloat16)
        block_up_gradient = (adapter_scale * jnp.dot(projected_up.T, output_rows, preferred_element_type=jnp.float32)).astype(jnp.bfloat16)
        return gradient_rows, block_down_gradient, block_up_gradient

    gradient_rows, block_down_gradient, block_up_gradient = lax.map(one_block, (hid_blocks, out_blocks, block_adapter_index))
    grad_hidden = gradient_rows.reshape(TOKENS, HIDDEN_WIDTH)
    grad_a = jax.ops.segment_sum(block_down_gradient.astype(jnp.float32), block_adapter_index, num_segments=ADAPTER_TOTAL)
    grad_b = jax.ops.segment_sum(block_up_gradient.astype(jnp.float32), block_adapter_index, num_segments=ADAPTER_TOTAL)
    return grad_hidden, grad_a.astype(jnp.bfloat16), grad_b.astype(jnp.bfloat16)
```

```python
import functools

import jax
import jax.numpy as jnp
from jax import lax
from jax.experimental import pallas as pl
from jax.experimental.pallas import tpu as pltpu
from jax.sharding import PartitionSpec as P

ADAPTER_RANK = 16
BLOCK = 128
CAP = 2
MESH = pl.DeviceIdType.MESH
NDP = 16
NCHIP = 8
NT = 16
NBLK = 8
OWNED = 32
SLOTS = 28
GROUP = 4
CHUNKS = SLOTS // GROUP
NFIN = 2 * SLOTS + 16
VMEM_LIMIT = 56 * 1024 * 1024


adapter_scale = 2.0


def general(hidden, output_gradient, block_adapter_index, adapter_down_factors, adapter_up_factors):
    dp_size = lax.axis_size("dp")
    my_index = lax.axis_index("dp")
    block_count = block_adapter_index.shape[0]
    owned_adapter_count = adapter_down_factors.shape[0]
    ff_local = hidden.shape[1]
    d_local = output_gradient.shape[1]
    slot_count = dp_size * CAP
    all_ids = lax.all_gather(block_adapter_index, "dp", axis=0, tiled=True).reshape(
        dp_size, block_count
    )
    owners = all_ids // owned_adapter_count
    local_ids = all_ids % owned_adapter_count
    same_owner = owners[:, :, None] == owners[:, None, :]
    block_range = jnp.arange(block_count, dtype=jnp.int32)
    earlier = block_range[None, :] < block_range[:, None]
    rank_in = jnp.sum(jnp.logical_and(same_owner, earlier[None, :, :]), axis=2)
    cap_range = jnp.arange(CAP, dtype=jnp.int32)
    chosen = jnp.logical_and(
        (owners == my_index)[:, None, :], rank_in[:, None, :] == cap_range[None, :, None]
    )
    owned_range = jnp.arange(owned_adapter_count, dtype=jnp.int32)
    local_match = local_ids[:, :, None] == owned_range[None, None, :]
    selection_table = jnp.sum(
        jnp.logical_and(chosen[:, :, :, None], local_match[:, None, :, :]), axis=2
    )
    selection_table = selection_table.reshape(slot_count, owned_adapter_count).astype(jnp.bfloat16)
    send_a = jnp.einsum(
        "dz,zeg->deg", selection_table, adapter_down_factors, preferred_element_type=jnp.float32
    ).astype(jnp.bfloat16)
    send_b = jnp.einsum(
        "ge,elq->glq", selection_table, adapter_up_factors, preferred_element_type=jnp.float32
    ).astype(jnp.bfloat16)
    send_a = send_a.reshape(dp_size, CAP, ADAPTER_RANK, ff_local)
    send_b = send_b.reshape(dp_size, CAP, ADAPTER_RANK, d_local)
    fetched_a, fetched_b = (
        lax.all_to_all(send_a, "dp", split_axis=0, concat_axis=0, tiled=True),
        lax.all_to_all(send_b, "dp", split_axis=0, concat_axis=0, tiled=True),
    )
    fetched_a = fetched_a.reshape(slot_count, ADAPTER_RANK, ff_local)
    fetched_b = fetched_b.reshape(slot_count, ADAPTER_RANK, d_local)
    my_owners = jnp.take(owners, my_index, axis=0)
    my_ranks = jnp.take(rank_in, my_index, axis=0)
    my_slots = my_owners * CAP + my_ranks
    down_factor = jnp.take(fetched_a, my_slots, axis=0)
    up_factor = jnp.take(fetched_b, my_slots, axis=0)
    hid_blocks = hidden.reshape(block_count, BLOCK, ff_local)
    out_blocks = output_gradient.reshape(block_count, BLOCK, d_local)
    proj_part = jnp.einsum(
        "jtf,jrf->jtr", hid_blocks, down_factor, preferred_element_type=jnp.float32
    )
    back_part = jnp.einsum(
        "jtd,jrd->jtr", out_blocks, up_factor, preferred_element_type=jnp.float32
    )
    proj, back = lax.psum((proj_part, back_part), "tensor")
    projected_up = proj.astype(jnp.bfloat16)
    backward_up = back.astype(jnp.bfloat16)
    block_down_gradient = (
        adapter_scale
        * jnp.einsum("jtr,jtf->jrf", backward_up, hid_blocks, preferred_element_type=jnp.float32)
    ).astype(jnp.bfloat16)
    block_up_gradient = (
        adapter_scale
        * jnp.einsum("jtr,jtd->jrd", projected_up, out_blocks, preferred_element_type=jnp.float32)
    ).astype(jnp.bfloat16)
    gradient_rows = adapter_scale * jnp.einsum(
        "jtr,jrf->jtf", backward_up, down_factor, preferred_element_type=jnp.float32
    )
    grad_hidden = gradient_rows.astype(jnp.bfloat16).reshape(block_count * BLOCK, ff_local)
    slot_range = jnp.arange(slot_count, dtype=jnp.int32)
    place_table = (slot_range[:, None] == my_slots[None, :]).astype(jnp.bfloat16)
    back_a = jnp.einsum(
        "kj,jrf->krf", place_table, block_down_gradient, preferred_element_type=jnp.float32
    ).astype(jnp.bfloat16)
    back_bb = jnp.einsum(
        "kj,jrd->krd", place_table, block_up_gradient, preferred_element_type=jnp.float32
    ).astype(jnp.bfloat16)
    back_a = back_a.reshape(dp_size, CAP, ADAPTER_RANK, ff_local)
    back_bb = back_bb.reshape(dp_size, CAP, ADAPTER_RANK, d_local)
    recv_a, recv_b = (
        lax.all_to_all(back_a, "dp", split_axis=0, concat_axis=0, tiled=True),
        lax.all_to_all(back_bb, "dp", split_axis=0, concat_axis=0, tiled=True),
    )
    sum_table = jnp.transpose(selection_table)
    grad_a = jnp.einsum(
        "ak,krf->arf",
        sum_table,
        recv_a.reshape(slot_count, ADAPTER_RANK, ff_local),
        preferred_element_type=jnp.float32,
    )
    grad_b = jnp.einsum(
        "ak,krd->ard",
        sum_table,
        recv_b.reshape(slot_count, ADAPTER_RANK, d_local),
        preferred_element_type=jnp.float32,
    )
    return (grad_hidden, grad_a.astype(jnp.bfloat16), grad_b.astype(jnp.bfloat16))


def bcast(x, shape=(8, 128)):
    return jnp.broadcast_to(x, shape)


def pick_row(x, sub, row):
    return bcast(jnp.sum(jnp.where(sub == row, x, 0), axis=0, keepdims=True))


def slot_plan(src, dst, own_index, chip, sub, lane):
    ahead = (dst - src) & 7
    tie = lane & 1
    plus = jnp.logical_and(ahead > 0, jnp.logical_or(ahead < 4, jnp.logical_and(ahead == 4, tie == 0)))
    minus = jnp.logical_or(ahead > 4, jnp.logical_and(ahead == 4, tie == 1))
    dist = jnp.where(plus, ahead, jnp.where(minus, 8 - ahead, 0))
    group = jnp.where(ahead > 0, src * 2 + jnp.where(minus, 1, 0), 16)
    order = group * 1024 + (4 - dist) * 128 + lane
    row = jnp.concatenate([order] * 16, axis=0)
    col = jnp.transpose(row)
    before = jnp.logical_and((row >> 10) == (col >> 10), col < row)
    rank = bcast(jnp.sum(jnp.where(before, 1, 0), axis=0, keepdims=True))
    result = []
    longest = jnp.zeros((8, 128), jnp.int32)
    for sign, act in ((1, plus), (-1, minus)):
        def shifted(x, by):
            by = (sign * by) % 8
            return pltpu.roll(x, by, 0) if by else x

        counts = [
            bcast(
                jnp.sum(
                    jnp.where(jnp.logical_and(jnp.logical_and(src == sub, act), dist > h), 1, 0),
                    axis=1,
                    keepdims=True,
                )
            )
            for h in range(4)
        ]
        starts = [jnp.zeros((8, 128), jnp.int32)]
        for h in range(1, 4):
            starts.append(
                jnp.maximum(
                    starts[h - 1] + shifted(counts[h - 1], h - 1),
                    shifted(starts[h - 1], 1) + GROUP,
                )
            )
        for h in range(4):
            here = shifted(counts[h], h)
            longest = jnp.maximum(longest, jnp.where(here > 0, starts[h] + here, 0))
        age = (sign * (chip - src)) & 7
        out_start = jnp.zeros((8, 128), jnp.int32)
        in_start = jnp.zeros((8, 128), jnp.int32)
        before_chip = (chip - sign) & 7
        for h in range(4):
            out_start = jnp.where(age == h, pick_row(starts[h], sub, chip), out_start)
            in_start = jnp.where(age == h + 1, pick_row(starts[h], sub, before_chip), in_start)
        leaves = jnp.logical_and(act, age < dist)
        arrives = jnp.logical_and(act, age == dist)
        out_slot = out_start + rank
        in_slot = in_start + rank
        source = jnp.where(age == 0, own_index + 1, 65 + in_slot)
        result.append((leaves, out_slot, source, arrives, in_slot))
    return result, longest


def by_row(mask, place, value, rows):
    reps = rows // 8
    wide = [jnp.concatenate([v] * reps, axis=0) for v in (jnp.where(mask, place, -1), value)]
    sub = lax.broadcasted_iota(jnp.int32, (rows, 128), 0)
    return jnp.sum(jnp.where(wide[0] == sub, wide[1], 0), axis=1, keepdims=True)


def make_tables(ids, me):
    chip = me // 2
    sub = lax.broadcasted_iota(jnp.int32, (8, 128), 0)
    lane = lax.broadcasted_iota(jnp.int32, (8, 128), 1)
    token_chip = lane >> 4
    owner_chip = ids >> 6
    chip_slot = ids & 63
    mine = (ids >> 5) == me
    row = (ids & 31) + 1
    fetch, longest_f = slot_plan(owner_chip, token_chip, chip_slot, chip, sub, lane)
    back, longest_b = slot_plan(token_chip, owner_chip, lane & 15, chip, sub, lane)
    fits = jnp.max(jnp.maximum(longest_f, longest_b), axis=0, keepdims=True) <= SLOTS
    columns = []
    for plan in (fetch, back):
        for leaves, out_slot, source, _, _ in plan:
            columns.append(by_row(leaves, out_slot, source, 32))
    where = jnp.where(owner_chip == token_chip, chip_slot + 1, 0)
    for d in range(2):
        where = jnp.where(fetch[d][3], 65 + d * SLOTS + fetch[d][4], where)
    columns.append(by_row((lane >> 3) == me, lane & 7, where, 32))
    for d in range(2):
        columns.append(by_row(jnp.logical_and(back[d][3], mine), back[d][4], row, 32))
    stays = jnp.logical_and(jnp.logical_and(owner_chip == token_chip, token_chip == chip), mine)
    columns.append(by_row(stays, lane & 15, row, 32))
    wide_lane = lax.broadcasted_iota(jnp.int32, (32, 128), 1)
    table = jnp.where(jnp.broadcast_to(fits, (32, 128)), 1, 0)
    for i, column in enumerate(columns):
        table = jnp.where(wide_lane == i, jnp.broadcast_to(column, (32, 128)), table)
    return table


def wait_bytes(ref, sem):
    pltpu.make_async_copy(ref, ref, sem).wait()


def ring_kernel(hw, dw, ids_ref, hid_hbm, og_hbm, a_hbm, b_hbm, table_ref, fac, pb, fin,
                idbuf, table, own_r, own_s, picked, stage, hid, og, part, parts, grads, items, arrivals,
                loc, ids_sem, sib, ring_send, ring_recv, fwd, psum_sem):
    half = hw + dw
    pieces = ((0, 640), (640, half - 640))
    me = lax.axis_index("dp")
    t = lax.axis_index("tensor")
    chip = me // 2
    core = me % 2
    other = 1 - core
    sibling = {"dp": chip * 2 + other}
    ko = pl.multiple_of(core * half, 128)
    so = pl.multiple_of(other * half, 128)
    mine32 = pl.ds(pl.multiple_of(core * OWNED, OWNED), OWNED)
    mine8 = pl.ds(pl.multiple_of(core * NBLK, NBLK), NBLK)

    def far(src, dst, send, recv, where):
        return pltpu.make_async_remote_copy(
            src_ref=src, dst_ref=dst, send_sem=send, recv_sem=recv, device_id=where, device_id_type=MESH
        )

    def cut(ref, width, which):
        return ref.at[:, :, pl.ds(pl.multiple_of(which * width, 128), width)]

    for ref, dst, width, at in ((a_hbm, own_r, hw, 0), (b_hbm, own_r, dw, hw)):
        pltpu.make_async_copy(cut(ref, width, core), dst.at[mine32, :, pl.ds(at, width)], loc.at[0]).start()
    for ref, dst, width, at in ((a_hbm, own_s, hw, 0), (b_hbm, own_s, dw, hw)):
        pltpu.make_async_copy(cut(ref, width, other), dst.at[mine32, :, pl.ds(at, width)], loc.at[1]).start()
    pltpu.make_async_copy(hid_hbm, hid, loc.at[2]).start()
    pltpu.make_async_copy(og_hbm, og, loc.at[3]).start()

    barrier = pltpu.get_barrier_semaphore()
    for o in range(1, NDP):
        pl.semaphore_signal(barrier, inc=1, device_id={"dp": lax.rem(me + o, NDP)}, device_id_type=MESH)
    for o in range(1, NT):
        pl.semaphore_signal(barrier, inc=1, device_id={"tensor": lax.rem(t + o, NT)}, device_id_type=MESH)
    lane = lax.broadcasted_iota(jnp.int32, (8, 128), 1)
    idbuf[me] = jnp.where((lane >> 3) == me, ids_ref[...], 0)
    pl.semaphore_wait(barrier, NDP - 1 + NT - 1)

    for o in range(1, NDP):
        far(idbuf.at[me], idbuf.at[me], ids_sem.at[0], ids_sem.at[1], {"dp": lax.rem(me + o, NDP)}).start()
    for ref, width, at in ((a_hbm, hw, 0), (b_hbm, dw, hw)):
        far(cut(ref, width, other), own_r.at[mine32, :, pl.ds(at, width)], sib.at[0], sib.at[1], sibling).start()
    for ref, width, at in ((a_hbm, hw, 0), (b_hbm, dw, hw)):
        far(cut(ref, width, core), own_s.at[mine32, :, pl.ds(at, width)], sib.at[2], sib.at[3], sibling).start()

    wait_bytes(idbuf.at[pl.ds(0, NDP - 1)], ids_sem.at[1])
    ids = idbuf[0]
    for i in range(1, NDP):
        ids = ids + idbuf[i]
    table_ref[...] = make_tables(ids, me)
    to_smem = pltpu.make_async_copy(table_ref, table, loc.at[4])
    to_smem.start()
    to_smem.wait()

    def ring(phase, own, count, land):
        def chunk(d, q, p):
            return arrivals[((phase * 2 + d) * CHUNKS + q) * 2 + p]

        def copy(d, q, p):
            at, width = pieces[p]
            return far(
                stage.at[phase, d, pl.ds(q * GROUP, GROUP), :, pl.ds(at, width)],
                chunk(d, q, p),
                ring_send.at[phase],
                ring_recv.at[phase, d, q, p],
                {"dp": lax.rem(chip + (1 if d == 0 else NCHIP - 1), NCHIP) * 2 + core},
            )

        def landed(d, q, p):
            at, width = pieces[p]
            copy(d, q, p).wait_recv()
            there = land.at[
                pl.ds(d * SLOTS + q * GROUP, GROUP), :, pl.ds(pl.multiple_of(ko + at, 128), width)
            ]
            pltpu.make_async_copy(chunk(d, q, p), there, fwd.at[phase, 0]).start()
            far(chunk(d, q, p), there, fwd.at[phase, 1], fwd.at[phase, 2], sibling).start()

        for m in range(CHUNKS):
            for p in range(2):
                at, width = pieces[p]
                for d in range(2):
                    if m > 0:
                        landed(d, m - 1, p)
                    for i in range(GROUP):
                        code = table[m * GROUP + i, phase * 2 + d]
                        value = own[jnp.clip(code - 1, 0, count - 1), :, pl.ds(at, width)]
                        for q in range(m):
                            place = code - 65 - q * GROUP
                            inside = jnp.logical_and(place >= 0, place < GROUP)
                            value = jnp.where(inside, chunk(d, q, p)[jnp.clip(place, 0, GROUP - 1)], value)
                        stage[phase, d, m * GROUP + i, :, pl.ds(at, width)] = value
                    copy(d, m, p).start()
        for p in range(2):
            for d in range(2):
                landed(d, CHUNKS - 1, p)
        everything = land.at[pl.ds(0, 2 * SLOTS), :, pl.ds(0, half)]
        wait_bytes(everything, fwd.at[phase, 0])
        wait_bytes(everything, fwd.at[phase, 2])

    wait_bytes(own_r.at[pl.ds(0, OWNED)], loc.at[0])
    wait_bytes(own_r.at[pl.ds(0, OWNED)], sib.at[1])
    ring(0, own_r, 2 * OWNED, picked)
    wait_bytes(own_s.at[pl.ds(0, OWNED)], loc.at[1])
    wait_bytes(own_s.at[pl.ds(0, OWNED)], sib.at[3])

    for j in range(NBLK):
        code = table[j, 4]
        near = code <= 64
        at = jnp.clip(code - 1, 0, 2 * OWNED - 1)
        away = jnp.clip(code - 65, 0, 2 * SLOTS - 1)
        for own, o in ((own_r, ko), (own_s, so)):
            fac[j, :, pl.ds(o, half)] = jnp.where(near, own[at], picked[away, :, pl.ds(o, half)])

    wait_bytes(hid, loc.at[2])
    wait_bytes(og, loc.at[3])
    for j in range(NBLK):
        rows = pl.ds(j * BLOCK, BLOCK)
        for i, ref, base, width in ((j, hid, 0, hw), (NBLK + j, og, hw, dw)):
            total = None
            for h in range(2):
                term = lax.dot_general(
                    fac[j, :, pl.ds(h * half + base, width)],
                    ref[rows, pl.ds(h * width, width)],
                    (((1,), (1,)), ((), ())),
                    preferred_element_type=jnp.float32,
                )
                total = term if total is None else total + term
            part[i] = total

    parts[t] = part[t]
    for o in range(1, NT):
        peer = lax.rem(t + o, NT)
        far(part.at[peer], parts.at[t], psum_sem.at[0], psum_sem.at[1], {"tensor": peer}).start()
    wait_bytes(parts.at[pl.ds(0, NT - 1)], psum_sem.at[1])
    total = parts[0]
    for i in range(1, NT):
        total = total + parts[i]
    pb[t] = total.astype(jnp.bfloat16)
    for o in range(1, NT):
        peer = lax.rem(t + o, NT)
        far(pb.at[t], pb.at[t], psum_sem.at[2], psum_sem.at[3], {"tensor": peer}).start()
    wait_bytes(pb.at[pl.ds(0, NT - 1)], psum_sem.at[3])

    for j in range(NBLK):
        rows = pl.ds(j * BLOCK, BLOCK)
        for i, ref, base, width in ((NBLK + j, hid, 0, hw), (j, og, hw, dw)):
            for h in range(2):
                grad = adapter_scale * jnp.dot(
                    pb[i], ref[rows, pl.ds(h * width, width)], preferred_element_type=jnp.float32
                )
                grads[j, :, pl.ds(h * half + base, width)] = grad.astype(jnp.bfloat16)
    swap = far(grads.at[:, :, pl.ds(so, half)], items.at[mine8], sib.at[4], sib.at[5], sibling)
    swap.start()
    keep = pltpu.make_async_copy(
        grads, fin.at[pl.ds(pl.multiple_of(2 * SLOTS + core * NBLK, NBLK), NBLK)], loc.at[5]
    )
    keep.start()
    share = far(
        grads, fin.at[pl.ds(pl.multiple_of(2 * SLOTS + core * NBLK, NBLK), NBLK)], sib.at[6], sib.at[7], sibling
    )
    share.start()
    items[mine8] = grads[:, :, pl.ds(ko, half)]
    swap.wait_recv()
    ring(1, items, 2 * NBLK, fin)

    keep.wait()
    share.wait()
    swap.wait_send()
    wait_bytes(idbuf.at[pl.ds(0, NDP - 1)], ids_sem.at[0])
    wait_bytes(own_r.at[pl.ds(0, OWNED)], sib.at[0])
    wait_bytes(own_s.at[pl.ds(0, OWNED)], sib.at[2])
    wait_bytes(parts.at[pl.ds(0, NT - 1)], psum_sem.at[0])
    wait_bytes(pb.at[pl.ds(0, NT - 1)], psum_sem.at[2])
    for phase in range(2):
        wait_bytes(stage.at[phase], ring_send.at[phase])
        wait_bytes(picked.at[pl.ds(0, 2 * SLOTS), :, pl.ds(0, half)], fwd.at[phase, 1])


def last_kernel(hw, dw, table, fin, fac, pb, gh, ga, gb, acc, buf, ghb, gab, gbb, sems):
    half = hw + dw

    def code_of(p):
        column = jnp.where(p < SLOTS, 5, jnp.where(p < 2 * SLOTS, 6, 7))
        row = jnp.where(p < SLOTS, p, jnp.where(p < 2 * SLOTS, p - SLOTS, p - 2 * SLOTS))
        return table[row, column]

    def fetch(p, carry):
        @pl.when(code_of(p) > 0)
        def _():
            pltpu.make_async_copy(fin.at[p], buf.at[p], sems.at[0]).start()

        return carry

    lax.fori_loop(0, NFIN, fetch, 0)
    for j in range(NBLK):
        rows = pl.ds(j * BLOCK, BLOCK)
        for h in range(2):
            rows_out = adapter_scale * lax.dot_general(
                pb[NBLK + j],
                fac[j, :, pl.ds(h * half, hw)],
                (((0,), (0,)), ((), ())),
                preferred_element_type=jnp.float32,
            )
            ghb[rows, pl.ds(h * hw, hw)] = rows_out.astype(jnp.bfloat16)
        pltpu.make_async_copy(ghb.at[rows], gh.at[rows], sems.at[1]).start()
    acc[...] = jnp.zeros_like(acc)

    def drain(p, carry):
        @pl.when(code_of(p) > 0)
        def _():
            pltpu.make_async_copy(fin.at[p], buf.at[p], sems.at[0]).wait()

        return carry

    lax.fori_loop(0, NFIN, drain, 0)

    def add(p, carry):
        code = code_of(p)

        @pl.when(code > 0)
        def _():
            acc[code - 1] += buf[p].astype(jnp.float32)

        return carry

    lax.fori_loop(0, NFIN, add, 0)

    def write(i, carry):
        for h in range(2):
            gab[i, :, pl.ds(h * hw, hw)] = acc[i, :, pl.ds(h * half, hw)].astype(jnp.bfloat16)
            gbb[i, :, pl.ds(h * dw, dw)] = acc[i, :, pl.ds(h * half + hw, dw)].astype(jnp.bfloat16)
        return carry

    lax.fori_loop(0, OWNED, write, 0)
    ca = pltpu.make_async_copy(gab, ga, sems.at[2])
    cb = pltpu.make_async_copy(gbb, gb, sems.at[3])
    ca.start()
    cb.start()
    pltpu.make_async_copy(ghb, gh, sems.at[1]).wait()
    ca.wait()
    cb.wait()


def shards(hidden, output_gradient, block_adapter_index, adapter_down_factors, adapter_up_factors):
    rows, ff_local = hidden.shape
    d_local = output_gradient.shape[1]
    hw, dw = ff_local // 2, d_local // 2
    half = hw + dw
    wide_ids = jnp.broadcast_to(jnp.tile(block_adapter_index, 16)[None, :], (8, 128))
    bf16, f32 = jnp.bfloat16, jnp.float32
    vmem = pl.BlockSpec(memory_space=pltpu.VMEM)
    anywhere = pl.BlockSpec(memory_space=pl.ANY)
    dma = pltpu.SemaphoreType.DMA
    chunk_shapes = [
        pltpu.VMEM((GROUP, ADAPTER_RANK, width), bf16) for _ in range(4 * CHUNKS) for width in (640, half - 640)
    ]
    scratch = [
        pltpu.VMEM((NDP, 8, 128), jnp.int32),
        pltpu.SMEM((32, 128), jnp.int32),
        pltpu.VMEM((2 * OWNED, ADAPTER_RANK, half), bf16),
        pltpu.VMEM((2 * OWNED, ADAPTER_RANK, half), bf16),
        pltpu.VMEM((2 * SLOTS, ADAPTER_RANK, 2 * half), bf16),
        pltpu.VMEM((2, 2, SLOTS, ADAPTER_RANK, half), bf16),
        pltpu.VMEM((rows, ff_local), bf16),
        pltpu.VMEM((rows, d_local), bf16),
        pltpu.VMEM((2 * NBLK, ADAPTER_RANK, BLOCK), f32),
        pltpu.VMEM((NT, ADAPTER_RANK, BLOCK), f32),
        pltpu.VMEM((NBLK, ADAPTER_RANK, 2 * half), bf16),
        pltpu.VMEM((2 * NBLK, ADAPTER_RANK, half), bf16),
    ]
    sems = [
        dma((6,)),
        dma((2,)),
        dma((8,)),
        dma((2,)),
        dma((2, 2, CHUNKS, 2)),
        dma((2, 3)),
        dma((4,)),
    ]
    n_scratch, n_chunks = len(scratch), len(chunk_shapes)

    def body(*refs):
        head = 9 + n_scratch
        ring_kernel(hw, dw, *refs[:head], refs[head : head + n_chunks], *refs[head + n_chunks :])

    table, fac, pb, fin = pl.pallas_call(
        body,
        name="ring",
        out_shape=(
            jax.ShapeDtypeStruct((32, 128), jnp.int32),
            jax.ShapeDtypeStruct((NBLK, ADAPTER_RANK, 2 * half), bf16),
            jax.ShapeDtypeStruct((2 * NBLK, ADAPTER_RANK, BLOCK), bf16),
            jax.ShapeDtypeStruct((NFIN, ADAPTER_RANK, 2 * half), bf16),
        ),
        in_specs=[vmem, anywhere, anywhere, anywhere, anywhere],
        out_specs=(vmem, vmem, vmem, anywhere),
        scratch_shapes=scratch + chunk_shapes + sems,
        compiler_params=pltpu.CompilerParams(
            collective_id=0, has_side_effects=True, vmem_limit_bytes=VMEM_LIMIT
        ),
    )(wide_ids, hidden, output_gradient, adapter_down_factors, adapter_up_factors)

    def finish(*_):
        return pl.pallas_call(
            functools.partial(last_kernel, hw, dw),
            name="finish",
            out_shape=(
                jax.ShapeDtypeStruct((rows, ff_local), bf16),
                jax.ShapeDtypeStruct(adapter_down_factors.shape, bf16),
                jax.ShapeDtypeStruct(adapter_up_factors.shape, bf16),
            ),
            in_specs=[pl.BlockSpec(memory_space=pltpu.SMEM), anywhere, vmem, vmem],
            out_specs=(anywhere, anywhere, anywhere),
            scratch_shapes=[
                pltpu.VMEM((OWNED, ADAPTER_RANK, 2 * half), f32),
                pltpu.VMEM((NFIN, ADAPTER_RANK, 2 * half), bf16),
                pltpu.VMEM((rows, ff_local), bf16),
                pltpu.VMEM((OWNED, ADAPTER_RANK, ff_local), bf16),
                pltpu.VMEM((OWNED, ADAPTER_RANK, d_local), bf16),
                dma((4,)),
            ],
            compiler_params=pltpu.CompilerParams(vmem_limit_bytes=VMEM_LIMIT),
        )(table, fin, fac, pb)

    return lax.cond(
        table[0, 8] > 0,
        finish,
        general,
        hidden,
        output_gradient,
        block_adapter_index,
        adapter_down_factors,
        adapter_up_factors,
    )


def solution(mesh):
    placed = (
        P("dp", "tensor"),
        P("dp", "tensor"),
        P("dp"),
        P("dp", None, "tensor"),
        P("dp", None, "tensor"),
    )
    return jax.shard_map(
        shards,
        mesh=mesh,
        in_specs=placed,
        out_specs=(P("dp", "tensor"), P("dp", None, "tensor"), P("dp", None, "tensor")),
        check_vma=False,
    )
```

```python
import functools

import jax
import jax.numpy as jnp
from jax import lax
from jax.experimental import pallas as pl
from jax.experimental.pallas import tpu as pltpu
from jax.sharding import PartitionSpec as P

ADAPTER_RANK = 16
BLOCK = 128
CAP = 2
MESH = pl.DeviceIdType.MESH
NDP = 16
NCHIP = 8
NT = 16
NBLK = 8
OWNED = 32
SLOTS = 28
GROUP = 2
BEHIND = 3
LAG = GROUP * BEHIND
CHUNKS = SLOTS // GROUP
NFIN = 2 * SLOTS + 16
VMEM_LIMIT = 56 * 1024 * 1024


adapter_scale = 2.0


def general(hidden, output_gradient, block_adapter_index, adapter_down_factors, adapter_up_factors):
    dp_size = lax.axis_size("dp")
    my_index = lax.axis_index("dp")
    block_count = block_adapter_index.shape[0]
    owned_adapter_count = adapter_down_factors.shape[0]
    ff_local = hidden.shape[1]
    d_local = output_gradient.shape[1]
    slot_count = dp_size * CAP
    all_ids = lax.all_gather(block_adapter_index, "dp", axis=0, tiled=True).reshape(
        dp_size, block_count
    )
    owners = all_ids // owned_adapter_count
    local_ids = all_ids % owned_adapter_count
    same_owner = owners[:, :, None] == owners[:, None, :]
    block_range = jnp.arange(block_count, dtype=jnp.int32)
    earlier = block_range[None, :] < block_range[:, None]
    rank_in = jnp.sum(jnp.logical_and(same_owner, earlier[None, :, :]), axis=2)
    cap_range = jnp.arange(CAP, dtype=jnp.int32)
    chosen = jnp.logical_and(
        (owners == my_index)[:, None, :], rank_in[:, None, :] == cap_range[None, :, None]
    )
    owned_range = jnp.arange(owned_adapter_count, dtype=jnp.int32)
    local_match = local_ids[:, :, None] == owned_range[None, None, :]
    selection_table = jnp.sum(
        jnp.logical_and(chosen[:, :, :, None], local_match[:, None, :, :]), axis=2
    )
    selection_table = selection_table.reshape(slot_count, owned_adapter_count).astype(jnp.bfloat16)
    send_a = jnp.einsum(
        "dz,zeg->deg", selection_table, adapter_down_factors, preferred_element_type=jnp.float32
    ).astype(jnp.bfloat16)
    send_b = jnp.einsum(
        "ge,elq->glq", selection_table, adapter_up_factors, preferred_element_type=jnp.float32
    ).astype(jnp.bfloat16)
    send_a = send_a.reshape(dp_size, CAP, ADAPTER_RANK, ff_local)
    send_b = send_b.reshape(dp_size, CAP, ADAPTER_RANK, d_local)
    fetched_a, fetched_b = (
        lax.all_to_all(send_a, "dp", split_axis=0, concat_axis=0, tiled=True),
        lax.all_to_all(send_b, "dp", split_axis=0, concat_axis=0, tiled=True),
    )
    fetched_a = fetched_a.reshape(slot_count, ADAPTER_RANK, ff_local)
    fetched_b = fetched_b.reshape(slot_count, ADAPTER_RANK, d_local)
    my_owners = jnp.take(owners, my_index, axis=0)
    my_ranks = jnp.take(rank_in, my_index, axis=0)
    my_slots = my_owners * CAP + my_ranks
    down_factor = jnp.take(fetched_a, my_slots, axis=0)
    up_factor = jnp.take(fetched_b, my_slots, axis=0)
    hid_blocks = hidden.reshape(block_count, BLOCK, ff_local)
    out_blocks = output_gradient.reshape(block_count, BLOCK, d_local)
    proj_part = jnp.einsum(
        "jtf,jrf->jtr", hid_blocks, down_factor, preferred_element_type=jnp.float32
    )
    back_part = jnp.einsum(
        "jtd,jrd->jtr", out_blocks, up_factor, preferred_element_type=jnp.float32
    )
    proj, back = lax.psum((proj_part, back_part), "tensor")
    projected_up = proj.astype(jnp.bfloat16)
    backward_up = back.astype(jnp.bfloat16)
    block_down_gradient = (
        adapter_scale
        * jnp.einsum("jtr,jtf->jrf", backward_up, hid_blocks, preferred_element_type=jnp.float32)
    ).astype(jnp.bfloat16)
    block_up_gradient = (
        adapter_scale
        * jnp.einsum("jtr,jtd->jrd", projected_up, out_blocks, preferred_element_type=jnp.float32)
    ).astype(jnp.bfloat16)
    gradient_rows = adapter_scale * jnp.einsum(
        "jtr,jrf->jtf", backward_up, down_factor, preferred_element_type=jnp.float32
    )
    grad_hidden = gradient_rows.astype(jnp.bfloat16).reshape(block_count * BLOCK, ff_local)
    slot_range = jnp.arange(slot_count, dtype=jnp.int32)
    place_table = (slot_range[:, None] == my_slots[None, :]).astype(jnp.bfloat16)
    back_a = jnp.einsum(
        "kj,jrf->krf", place_table, block_down_gradient, preferred_element_type=jnp.float32
    ).astype(jnp.bfloat16)
    back_bb = jnp.einsum(
        "kj,jrd->krd", place_table, block_up_gradient, preferred_element_type=jnp.float32
    ).astype(jnp.bfloat16)
    back_a = back_a.reshape(dp_size, CAP, ADAPTER_RANK, ff_local)
    back_bb = back_bb.reshape(dp_size, CAP, ADAPTER_RANK, d_local)
    recv_a, recv_b = (
        lax.all_to_all(back_a, "dp", split_axis=0, concat_axis=0, tiled=True),
        lax.all_to_all(back_bb, "dp", split_axis=0, concat_axis=0, tiled=True),
    )
    sum_table = jnp.transpose(selection_table)
    grad_a = jnp.einsum(
        "ak,krf->arf",
        sum_table,
        recv_a.reshape(slot_count, ADAPTER_RANK, ff_local),
        preferred_element_type=jnp.float32,
    )
    grad_b = jnp.einsum(
        "ak,krd->ard",
        sum_table,
        recv_b.reshape(slot_count, ADAPTER_RANK, d_local),
        preferred_element_type=jnp.float32,
    )
    return (grad_hidden, grad_a.astype(jnp.bfloat16), grad_b.astype(jnp.bfloat16))


def bcast(x, shape=(8, 128)):
    return jnp.broadcast_to(x, shape)


def pick_row(x, sub, row):
    return bcast(jnp.sum(jnp.where(sub == row, x, 0), axis=0, keepdims=True))


def slot_plan(src, dst, own_index, chip, sub, lane):
    ahead = (dst - src) & 7
    tie = lane & 1
    plus = jnp.logical_and(ahead > 0, jnp.logical_or(ahead < 4, jnp.logical_and(ahead == 4, tie == 0)))
    minus = jnp.logical_or(ahead > 4, jnp.logical_and(ahead == 4, tie == 1))
    dist = jnp.where(plus, ahead, jnp.where(minus, 8 - ahead, 0))
    group = jnp.where(ahead > 0, src * 2 + jnp.where(minus, 1, 0), 16)
    order = group * 1024 + (4 - dist) * 128 + lane
    row = jnp.concatenate([order] * 16, axis=0)
    col = jnp.transpose(row)
    before = jnp.logical_and((row >> 10) == (col >> 10), col < row)
    rank = bcast(jnp.sum(jnp.where(before, 1, 0), axis=0, keepdims=True))
    result = []
    longest = jnp.zeros((8, 128), jnp.int32)
    for sign, act in ((1, plus), (-1, minus)):
        def shifted(x, by):
            by = (sign * by) % 8
            return pltpu.roll(x, by, 0) if by else x

        counts = [
            bcast(
                jnp.sum(
                    jnp.where(jnp.logical_and(jnp.logical_and(src == sub, act), dist > h), 1, 0),
                    axis=1,
                    keepdims=True,
                )
            )
            for h in range(4)
        ]
        starts = [jnp.zeros((8, 128), jnp.int32)]
        for h in range(1, 4):
            starts.append(
                jnp.maximum(
                    starts[h - 1] + shifted(counts[h - 1], h - 1),
                    shifted(starts[h - 1], 1) + LAG,
                )
            )
        for h in range(4):
            here = shifted(counts[h], h)
            longest = jnp.maximum(longest, jnp.where(here > 0, starts[h] + here, 0))
        age = (sign * (chip - src)) & 7
        out_start = jnp.zeros((8, 128), jnp.int32)
        in_start = jnp.zeros((8, 128), jnp.int32)
        before_chip = (chip - sign) & 7
        for h in range(4):
            out_start = jnp.where(age == h, pick_row(starts[h], sub, chip), out_start)
            in_start = jnp.where(age == h + 1, pick_row(starts[h], sub, before_chip), in_start)
        leaves = jnp.logical_and(act, age < dist)
        arrives = jnp.logical_and(act, age == dist)
        out_slot = out_start + rank
        in_slot = in_start + rank
        source = jnp.where(age == 0, own_index + 1, 65 + in_slot)
        result.append((leaves, out_slot, source, arrives, in_slot))
    return result, longest


def by_row(mask, place, value, rows):
    reps = rows // 8
    wide = [jnp.concatenate([v] * reps, axis=0) for v in (jnp.where(mask, place, -1), value)]
    sub = lax.broadcasted_iota(jnp.int32, (rows, 128), 0)
    return jnp.sum(jnp.where(wide[0] == sub, wide[1], 0), axis=1, keepdims=True)


def make_tables(ids, me):
    chip = me // 2
    sub = lax.broadcasted_iota(jnp.int32, (8, 128), 0)
    lane = lax.broadcasted_iota(jnp.int32, (8, 128), 1)
    token_chip = lane >> 4
    owner_chip = ids >> 6
    chip_slot = ids & 63
    mine = (ids >> 5) == me
    fetch, longest_f = slot_plan(owner_chip, token_chip, chip_slot, chip, sub, lane)
    back, longest_b = slot_plan(token_chip, owner_chip, lane & 15, chip, sub, lane)
    fits = jnp.max(jnp.maximum(longest_f, longest_b), axis=0, keepdims=True) <= SLOTS
    columns = []
    for plan in (fetch, back):
        for leaves, out_slot, source, _, _ in plan:
            columns.append(by_row(leaves, out_slot, source, 32))
    where = jnp.where(owner_chip == token_chip, chip_slot + 1, 0)
    for d in range(2):
        where = jnp.where(fetch[d][3], 65 + d * SLOTS + fetch[d][4], where)
    columns.append(by_row((lane >> 3) == me, lane & 7, where, 32))
    stays = jnp.logical_and(owner_chip == token_chip, token_chip == chip)
    landing = jnp.where(stays, 2 * SLOTS + (lane & 15), -1)
    for d in range(2):
        landing = jnp.where(back[d][3], d * SLOTS + back[d][4], landing)
    wanted = jnp.logical_and(landing >= 0, mine)
    count = bcast(jnp.sum(jnp.where(wanted, 1, 0), axis=1, keepdims=True))
    line = lax.broadcasted_iota(jnp.int32, (128, 128), 1)
    ahead = jnp.transpose(jnp.concatenate([jnp.where(wanted, lane, 128)] * 16, axis=0))
    rank = bcast(jnp.sum(jnp.where(ahead < line, 1, 0), axis=0, keepdims=True))
    entry = jnp.where(wanted, rank * 4096 + landing * 32 + (ids & 31), -1)
    entry = jnp.transpose(jnp.concatenate([entry] * 16, axis=0))
    listed = bcast(jnp.sum(jnp.where((entry >> 12) == line, entry & 4095, 0), axis=0, keepdims=True))
    wide_lane = lax.broadcasted_iota(jnp.int32, (32, 128), 1)
    table = jnp.where(jnp.broadcast_to(fits, (32, 128)), 1, 0)
    for i, column in enumerate(columns):
        table = jnp.where(wide_lane == i, jnp.broadcast_to(column, (32, 128)), table)
    return jnp.concatenate([table, jnp.where(sub == 0, listed, count)], axis=0)


def wait_bytes(ref, sem):
    pltpu.make_async_copy(ref, ref, sem).wait()


def ring_kernel(hw, dw, ids_ref, hid_hbm, og_hbm, a_hbm, b_hbm, table_ref, fac, pb, fin,
                idbuf, table, own_r, own_s, picked, stage, hid, og, part, parts, grads, items, arrived, kept,
                loc, ids_sem, sib, ring_send, ring_recv, fwd, psum_sem):
    half = hw + dw
    me = lax.axis_index("dp")
    t = lax.axis_index("tensor")
    chip = me // 2
    core = me % 2
    other = 1 - core
    sibling = {"dp": chip * 2 + other}
    ko = pl.multiple_of(core * half, 128)
    so = pl.multiple_of(other * half, 128)
    mine32 = pl.ds(pl.multiple_of(core * OWNED, OWNED), OWNED)
    mine8 = pl.ds(pl.multiple_of(core * NBLK, NBLK), NBLK)

    def far(src, dst, send, recv, where):
        return pltpu.make_async_remote_copy(
            src_ref=src, dst_ref=dst, send_sem=send, recv_sem=recv, device_id=where, device_id_type=MESH
        )

    def cut(ref, width, which):
        return ref.at[:, :, pl.ds(pl.multiple_of(which * width, 128), width)]

    barrier = pltpu.get_barrier_semaphore()
    for o in range(1, NDP):
        pl.semaphore_signal(barrier, inc=1, device_id={"dp": lax.rem(me + o, NDP)}, device_id_type=MESH)
    for o in range(1, NT):
        pl.semaphore_signal(barrier, inc=1, device_id={"tensor": lax.rem(t + o, NT)}, device_id_type=MESH)
    for ref, dst, width, at in ((a_hbm, own_r, hw, 0), (b_hbm, own_r, dw, hw)):
        pltpu.make_async_copy(cut(ref, width, core), dst.at[mine32, :, pl.ds(at, width)], loc.at[0]).start()
    for ref, dst, width, at in ((a_hbm, own_s, hw, 0), (b_hbm, own_s, dw, hw)):
        pltpu.make_async_copy(cut(ref, width, other), dst.at[mine32, :, pl.ds(at, width)], loc.at[1]).start()
    pltpu.make_async_copy(hid_hbm, hid, loc.at[2]).start()
    pltpu.make_async_copy(og_hbm, og, loc.at[3]).start()

    lane = lax.broadcasted_iota(jnp.int32, (8, 128), 1)
    mine_ids = jnp.zeros((8, 128), jnp.int32)
    for j in range(NBLK):
        mine_ids = jnp.where(lane == me * NBLK + j, ids_ref[j], mine_ids)
    idbuf[me] = mine_ids
    pl.semaphore_wait(barrier, NDP - 1 + NT - 1)

    for o in range(1, NDP):
        far(idbuf.at[me], idbuf.at[me], ids_sem.at[0], ids_sem.at[1], {"dp": lax.rem(me + o, NDP)}).start()
    for ref, width, at in ((a_hbm, hw, 0), (b_hbm, dw, hw)):
        far(cut(ref, width, other), own_r.at[mine32, :, pl.ds(at, width)], sib.at[0], sib.at[1], sibling).start()
    for ref, width, at in ((a_hbm, hw, 0), (b_hbm, dw, hw)):
        far(cut(ref, width, core), own_s.at[mine32, :, pl.ds(at, width)], sib.at[2], sib.at[3], sibling).start()

    wait_bytes(idbuf.at[pl.ds(0, NDP - 1)], ids_sem.at[1])
    ids = idbuf[0]
    for i in range(1, NDP):
        ids = ids + idbuf[i]
    table_ref[...] = make_tables(ids, me)
    to_smem = pltpu.make_async_copy(table_ref, table, loc.at[4])
    to_smem.start()
    to_smem.wait()

    def ring(phase, own, count, land):
        def copy(d, q):
            slots = pl.ds(q * GROUP, GROUP)
            return far(
                stage.at[phase, d, slots],
                arrived.at[phase, d, slots],
                ring_send.at[phase],
                ring_recv.at[phase, d, q],
                {"dp": lax.rem(chip + (1 if d == 0 else NCHIP - 1), NCHIP) * 2 + core},
            )

        def landed(d, q):
            copy(d, q).wait_recv()
            slots = pl.ds(q * GROUP, GROUP)
            there = land.at[pl.ds(d * SLOTS + q * GROUP, GROUP), :, pl.ds(ko, half)]
            far(arrived.at[phase, d, slots], there, fwd.at[phase, 1], fwd.at[phase, 2], sibling).start()
            if phase == 1:
                pltpu.make_async_copy(arrived.at[phase, d, slots], there, fwd.at[phase, 0]).start()
            kept[pl.ds(d * SLOTS + q * GROUP, GROUP)] = arrived[phase, d, slots]

        for m in range(CHUNKS + BEHIND):
            for d in range(2):
                if m >= BEHIND:
                    landed(d, m - BEHIND)
                if m < CHUNKS:
                    for i in range(GROUP):
                        code = table[m * GROUP + i, phase * 2 + d]
                        value = own[jnp.clip(code - 1, 0, count - 1)]
                        if m >= BEHIND:
                            passed = kept[d * SLOTS + jnp.clip(code - 65, 0, SLOTS - 1)]
                            value = jnp.where(code > 64, passed, value)
                        stage[phase, d, m * GROUP + i] = value
                    copy(d, m).start()
        everything = land.at[pl.ds(0, 2 * SLOTS), :, pl.ds(0, half)]
        if phase == 1:
            wait_bytes(everything, fwd.at[phase, 0])
        wait_bytes(everything, fwd.at[phase, 2])

    wait_bytes(own_r.at[pl.ds(0, OWNED)], loc.at[0])
    wait_bytes(own_r.at[pl.ds(0, OWNED)], sib.at[1])
    ring(0, own_r, 2 * OWNED, picked)
    wait_bytes(own_s.at[pl.ds(0, OWNED)], loc.at[1])
    wait_bytes(own_s.at[pl.ds(0, OWNED)], sib.at[3])

    for j in range(NBLK):
        code = table[j, 4]
        near = code <= 64
        at = jnp.clip(code - 1, 0, 2 * OWNED - 1)
        away = jnp.clip(code - 65, 0, 2 * SLOTS - 1)
        fac[j, :, pl.ds(ko, half)] = jnp.where(near, own_r[at], kept[away])
        fac[j, :, pl.ds(so, half)] = jnp.where(near, own_s[at], picked[away, :, pl.ds(so, half)])

    wait_bytes(hid, loc.at[2])
    wait_bytes(og, loc.at[3])
    for j in range(NBLK):
        rows = pl.ds(j * BLOCK, BLOCK)
        for i, ref, base, width in ((j, hid, 0, hw), (NBLK + j, og, hw, dw)):
            total = None
            for h in range(2):
                term = lax.dot_general(
                    fac[j, :, pl.ds(h * half + base, width)],
                    ref[rows, pl.ds(h * width, width)],
                    (((1,), (1,)), ((), ())),
                    preferred_element_type=jnp.float32,
                )
                total = term if total is None else total + term
            part[i] = total

    parts[t] = part[t]
    for o in range(1, NT):
        peer = lax.rem(t + o, NT)
        far(part.at[peer], parts.at[t], psum_sem.at[0], psum_sem.at[1], {"tensor": peer}).start()
    wait_bytes(parts.at[pl.ds(0, NT - 1)], psum_sem.at[1])
    total = parts[0]
    for i in range(1, NT):
        total = total + parts[i]
    pb[t] = total.astype(jnp.bfloat16)
    for o in range(1, NT):
        peer = lax.rem(t + o, NT)
        far(pb.at[t], pb.at[t], psum_sem.at[2], psum_sem.at[3], {"tensor": peer}).start()
    wait_bytes(pb.at[pl.ds(0, NT - 1)], psum_sem.at[3])

    for j in range(NBLK):
        rows = pl.ds(j * BLOCK, BLOCK)
        for i, ref, base, width in ((NBLK + j, hid, 0, hw), (j, og, hw, dw)):
            for h in range(2):
                grad = adapter_scale * jnp.dot(
                    pb[i], ref[rows, pl.ds(h * width, width)], preferred_element_type=jnp.float32
                )
                grads[j, :, pl.ds(h * half + base, width)] = grad.astype(jnp.bfloat16)
    swap = far(grads.at[:, :, pl.ds(so, half)], items.at[mine8], sib.at[4], sib.at[5], sibling)
    swap.start()
    keep = pltpu.make_async_copy(
        grads, fin.at[pl.ds(pl.multiple_of(2 * SLOTS + core * NBLK, NBLK), NBLK)], loc.at[5]
    )
    keep.start()
    share = far(
        grads, fin.at[pl.ds(pl.multiple_of(2 * SLOTS + core * NBLK, NBLK), NBLK)], sib.at[6], sib.at[7], sibling
    )
    share.start()
    items[mine8] = grads[:, :, pl.ds(ko, half)]
    swap.wait_recv()
    ring(1, items, 2 * NBLK, fin)

    keep.wait()
    share.wait()
    swap.wait_send()
    wait_bytes(idbuf.at[pl.ds(0, NDP - 1)], ids_sem.at[0])
    wait_bytes(own_r.at[pl.ds(0, OWNED)], sib.at[0])
    wait_bytes(own_s.at[pl.ds(0, OWNED)], sib.at[2])
    wait_bytes(parts.at[pl.ds(0, NT - 1)], psum_sem.at[0])
    wait_bytes(pb.at[pl.ds(0, NT - 1)], psum_sem.at[2])
    for phase in range(2):
        wait_bytes(stage.at[phase], ring_send.at[phase])
        wait_bytes(picked.at[pl.ds(0, 2 * SLOTS), :, pl.ds(0, half)], fwd.at[phase, 1])


def last_kernel(hw, dw, table, fin, fac, pb, gh, ga, gb, acc, buf, ghb, gab, gbb, sems):
    half = hw + dw
    count = table[33, 0]

    def arriving(p):
        return pltpu.make_async_copy(fin.at[table[32, p] >> 5], buf.at[p], sems.at[0])

    def loop(step):
        def run(p, carry):
            step(p)
            return carry

        lax.fori_loop(0, count, run, 0)

    loop(lambda p: arriving(p).start())
    for j in range(NBLK):
        rows = pl.ds(j * BLOCK, BLOCK)
        for h in range(2):
            rows_out = adapter_scale * lax.dot_general(
                pb[NBLK + j],
                fac[j, :, pl.ds(h * half, hw)],
                (((0,), (0,)), ((), ())),
                preferred_element_type=jnp.float32,
            )
            ghb[rows, pl.ds(h * hw, hw)] = rows_out.astype(jnp.bfloat16)
        pltpu.make_async_copy(ghb.at[rows], gh.at[rows], sems.at[1]).start()
    gab[...] = jnp.zeros_like(gab)
    gbb[...] = jnp.zeros_like(gbb)
    empty = jnp.zeros(acc.shape[1:], jnp.float32)

    def clear(p):
        acc[table[32, p] & 31] = empty

    def add(p):
        acc[table[32, p] & 31] += buf[p].astype(jnp.float32)

    def store(p):
        i = table[32, p] & 31
        for h in range(2):
            gab[i, :, pl.ds(h * hw, hw)] = acc[i, :, pl.ds(h * half, hw)].astype(jnp.bfloat16)
            gbb[i, :, pl.ds(h * dw, dw)] = acc[i, :, pl.ds(h * half + hw, dw)].astype(jnp.bfloat16)

    loop(clear)
    loop(lambda p: arriving(p).wait())
    loop(add)
    loop(store)
    ca = pltpu.make_async_copy(gab, ga, sems.at[2])
    cb = pltpu.make_async_copy(gbb, gb, sems.at[3])
    ca.start()
    cb.start()
    pltpu.make_async_copy(ghb, gh, sems.at[1]).wait()
    ca.wait()
    cb.wait()


def shards(hidden, output_gradient, block_adapter_index, adapter_down_factors, adapter_up_factors):
    rows, ff_local = hidden.shape
    d_local = output_gradient.shape[1]
    hw, dw = ff_local // 2, d_local // 2
    half = hw + dw
    bf16, f32 = jnp.bfloat16, jnp.float32
    vmem = pl.BlockSpec(memory_space=pltpu.VMEM)
    anywhere = pl.BlockSpec(memory_space=pl.ANY)
    dma = pltpu.SemaphoreType.DMA
    scratch = [
        pltpu.VMEM((NDP, 8, 128), jnp.int32),
        pltpu.SMEM((40, 128), jnp.int32),
        pltpu.VMEM((2 * OWNED, ADAPTER_RANK, half), bf16),
        pltpu.VMEM((2 * OWNED, ADAPTER_RANK, half), bf16),
        pltpu.VMEM((2 * SLOTS, ADAPTER_RANK, 2 * half), bf16),
        pltpu.VMEM((2, 2, SLOTS, ADAPTER_RANK, half), bf16),
        pltpu.VMEM((rows, ff_local), bf16),
        pltpu.VMEM((rows, d_local), bf16),
        pltpu.VMEM((2 * NBLK, ADAPTER_RANK, BLOCK), f32),
        pltpu.VMEM((NT, ADAPTER_RANK, BLOCK), f32),
        pltpu.VMEM((NBLK, ADAPTER_RANK, 2 * half), bf16),
        pltpu.VMEM((2 * NBLK, ADAPTER_RANK, half), bf16),
        pltpu.VMEM((2, 2, SLOTS, ADAPTER_RANK, half), bf16),
        pltpu.VMEM((2 * SLOTS, ADAPTER_RANK, half), bf16),
    ]
    sems = [
        dma((6,)),
        dma((2,)),
        dma((8,)),
        dma((2,)),
        dma((2, 2, CHUNKS)),
        dma((2, 3)),
        dma((4,)),
    ]
    table, fac, pb, fin = pl.pallas_call(
        functools.partial(ring_kernel, hw, dw),
        name="ring",
        out_shape=(
            jax.ShapeDtypeStruct((40, 128), jnp.int32),
            jax.ShapeDtypeStruct((NBLK, ADAPTER_RANK, 2 * half), bf16),
            jax.ShapeDtypeStruct((2 * NBLK, ADAPTER_RANK, BLOCK), bf16),
            jax.ShapeDtypeStruct((NFIN, ADAPTER_RANK, 2 * half), bf16),
        ),
        in_specs=[pl.BlockSpec(memory_space=pltpu.SMEM)] + [anywhere] * 4,
        out_specs=(vmem, vmem, vmem, anywhere),
        scratch_shapes=scratch + sems,
        compiler_params=pltpu.CompilerParams(
            collective_id=0, has_side_effects=True, vmem_limit_bytes=VMEM_LIMIT
        ),
    )(block_adapter_index, hidden, output_gradient, adapter_down_factors, adapter_up_factors)

    def finish(*_):
        return pl.pallas_call(
            functools.partial(last_kernel, hw, dw),
            name="finish",
            out_shape=(
                jax.ShapeDtypeStruct((rows, ff_local), bf16),
                jax.ShapeDtypeStruct(adapter_down_factors.shape, bf16),
                jax.ShapeDtypeStruct(adapter_up_factors.shape, bf16),
            ),
            in_specs=[pl.BlockSpec(memory_space=pltpu.SMEM), anywhere, vmem, vmem],
            out_specs=(anywhere, anywhere, anywhere),
            scratch_shapes=[
                pltpu.VMEM((OWNED, ADAPTER_RANK, 2 * half), f32),
                pltpu.VMEM((NFIN, ADAPTER_RANK, 2 * half), bf16),
                pltpu.VMEM((rows, ff_local), bf16),
                pltpu.VMEM((OWNED, ADAPTER_RANK, ff_local), bf16),
                pltpu.VMEM((OWNED, ADAPTER_RANK, d_local), bf16),
                dma((4,)),
            ],
            compiler_params=pltpu.CompilerParams(vmem_limit_bytes=VMEM_LIMIT),
        )(table, fin, fac, pb)

    return lax.cond(
        table[0, 8] > 0,
        finish,
        general,
        hidden,
        output_gradient,
        block_adapter_index,
        adapter_down_factors,
        adapter_up_factors,
    )


def solution(mesh):
    placed = (
        P("dp", "tensor"),
        P("dp", "tensor"),
        P("dp"),
        P("dp", None, "tensor"),
        P("dp", None, "tensor"),
    )
    return jax.shard_map(
        shards,
        mesh=mesh,
        in_specs=placed,
        out_specs=(P("dp", "tensor"), P("dp", None, "tensor"), P("dp", None, "tensor")),
        check_vma=False,
    )
```

```python
import functools

import jax
import jax.numpy as jnp
from jax import lax
from jax.experimental import pallas as pl
from jax.experimental.pallas import tpu as pltpu
from jax.sharding import PartitionSpec as P

ADAPTER_RANK = 16
BLOCK = 128
CAP = 2
MESH = pl.DeviceIdType.MESH
NDP = 16
NCHIP = 8
NT = 16
NBLK = 8
OWNED = 32
SLOTS_OUT = 25
SLOTS_BACK = 26
LAG = 6
NFIN = 2 * SLOTS_BACK + 16
ORDER_OUT = "bbbabbbababbababbababababaPaaaaRaa"
ORDER_BACK = "aaSaaaaGXbabbababbababbababbababbab"
VMEM_LIMIT = 56 * 1024 * 1024


adapter_scale = 2.0


def general(hidden, output_gradient, block_adapter_index, adapter_down_factors, adapter_up_factors):
    dp_size = lax.axis_size("dp")
    my_index = lax.axis_index("dp")
    block_count = block_adapter_index.shape[0]
    owned_adapter_count = adapter_down_factors.shape[0]
    ff_local = hidden.shape[1]
    d_local = output_gradient.shape[1]
    slot_count = dp_size * CAP
    all_ids = lax.all_gather(block_adapter_index, "dp", axis=0, tiled=True).reshape(
        dp_size, block_count
    )
    owners = all_ids // owned_adapter_count
    local_ids = all_ids % owned_adapter_count
    same_owner = owners[:, :, None] == owners[:, None, :]
    block_range = jnp.arange(block_count, dtype=jnp.int32)
    earlier = block_range[None, :] < block_range[:, None]
    rank_in = jnp.sum(jnp.logical_and(same_owner, earlier[None, :, :]), axis=2)
    cap_range = jnp.arange(CAP, dtype=jnp.int32)
    chosen = jnp.logical_and(
        (owners == my_index)[:, None, :], rank_in[:, None, :] == cap_range[None, :, None]
    )
    owned_range = jnp.arange(owned_adapter_count, dtype=jnp.int32)
    local_match = local_ids[:, :, None] == owned_range[None, None, :]
    selection_table = jnp.sum(
        jnp.logical_and(chosen[:, :, :, None], local_match[:, None, :, :]), axis=2
    )
    selection_table = selection_table.reshape(slot_count, owned_adapter_count).astype(jnp.bfloat16)
    send_a = jnp.einsum(
        "dz,zeg->deg", selection_table, adapter_down_factors, preferred_element_type=jnp.float32
    ).astype(jnp.bfloat16)
    send_b = jnp.einsum(
        "ge,elq->glq", selection_table, adapter_up_factors, preferred_element_type=jnp.float32
    ).astype(jnp.bfloat16)
    send_a = send_a.reshape(dp_size, CAP, ADAPTER_RANK, ff_local)
    send_b = send_b.reshape(dp_size, CAP, ADAPTER_RANK, d_local)
    fetched_a, fetched_b = (
        lax.all_to_all(send_a, "dp", split_axis=0, concat_axis=0, tiled=True),
        lax.all_to_all(send_b, "dp", split_axis=0, concat_axis=0, tiled=True),
    )
    fetched_a = fetched_a.reshape(slot_count, ADAPTER_RANK, ff_local)
    fetched_b = fetched_b.reshape(slot_count, ADAPTER_RANK, d_local)
    my_owners = jnp.take(owners, my_index, axis=0)
    my_ranks = jnp.take(rank_in, my_index, axis=0)
    my_slots = my_owners * CAP + my_ranks
    down_factor = jnp.take(fetched_a, my_slots, axis=0)
    up_factor = jnp.take(fetched_b, my_slots, axis=0)
    hid_blocks = hidden.reshape(block_count, BLOCK, ff_local)
    out_blocks = output_gradient.reshape(block_count, BLOCK, d_local)
    proj_part = jnp.einsum(
        "jtf,jrf->jtr", hid_blocks, down_factor, preferred_element_type=jnp.float32
    )
    back_part = jnp.einsum(
        "jtd,jrd->jtr", out_blocks, up_factor, preferred_element_type=jnp.float32
    )
    proj, back = lax.psum((proj_part, back_part), "tensor")
    projected_up = proj.astype(jnp.bfloat16)
    backward_up = back.astype(jnp.bfloat16)
    block_down_gradient = (
        adapter_scale
        * jnp.einsum("jtr,jtf->jrf", backward_up, hid_blocks, preferred_element_type=jnp.float32)
    ).astype(jnp.bfloat16)
    block_up_gradient = (
        adapter_scale
        * jnp.einsum("jtr,jtd->jrd", projected_up, out_blocks, preferred_element_type=jnp.float32)
    ).astype(jnp.bfloat16)
    gradient_rows = adapter_scale * jnp.einsum(
        "jtr,jrf->jtf", backward_up, down_factor, preferred_element_type=jnp.float32
    )
    grad_hidden = gradient_rows.astype(jnp.bfloat16).reshape(block_count * BLOCK, ff_local)
    slot_range = jnp.arange(slot_count, dtype=jnp.int32)
    place_table = (slot_range[:, None] == my_slots[None, :]).astype(jnp.bfloat16)
    back_a = jnp.einsum(
        "kj,jrf->krf", place_table, block_down_gradient, preferred_element_type=jnp.float32
    ).astype(jnp.bfloat16)
    back_bb = jnp.einsum(
        "kj,jrd->krd", place_table, block_up_gradient, preferred_element_type=jnp.float32
    ).astype(jnp.bfloat16)
    back_a = back_a.reshape(dp_size, CAP, ADAPTER_RANK, ff_local)
    back_bb = back_bb.reshape(dp_size, CAP, ADAPTER_RANK, d_local)
    recv_a, recv_b = (
        lax.all_to_all(back_a, "dp", split_axis=0, concat_axis=0, tiled=True),
        lax.all_to_all(back_bb, "dp", split_axis=0, concat_axis=0, tiled=True),
    )
    sum_table = jnp.transpose(selection_table)
    grad_a = jnp.einsum(
        "ak,krf->arf",
        sum_table,
        recv_a.reshape(slot_count, ADAPTER_RANK, ff_local),
        preferred_element_type=jnp.float32,
    )
    grad_b = jnp.einsum(
        "ak,krd->ard",
        sum_table,
        recv_b.reshape(slot_count, ADAPTER_RANK, d_local),
        preferred_element_type=jnp.float32,
    )
    return (grad_hidden, grad_a.astype(jnp.bfloat16), grad_b.astype(jnp.bfloat16))


def bcast(x, shape=(8, 128)):
    return jnp.broadcast_to(x, shape)


def pick_row(x, sub, row):
    return bcast(jnp.sum(jnp.where(sub == row, x, 0), axis=0, keepdims=True))


def turn(x, by):
    by = by % 8
    return pltpu.roll(x, by, 0) if by else x


def tall(x):
    return jnp.concatenate([x] * 16, axis=0)


def slot_plan(src, dst, own_index, shared, chip, sub, lane):
    ahead = (dst - src) & 7
    low = lax.broadcasted_iota(jnp.int32, (128, 128), 0)
    line = lax.broadcasted_iota(jnp.int32, (128, 128), 1)

    def per_chip(mask):
        return bcast(jnp.sum(jnp.where(jnp.logical_and(src == sub, mask), 1, 0), axis=1, keepdims=True))

    def over_all(x):
        return bcast(jnp.sum(x, axis=0, keepdims=True))

    one, two, three, across, five, six, seven = [per_chip(ahead == d) for d in range(1, 8)]
    load_p = one + two + three + turn(two + three, 1) + turn(three, 2)
    load_m = seven + six + five + turn(six + five, -1) + turn(five, -2)
    forward = jnp.zeros((8, 128), jnp.int32)
    for phase in range(4):
        worst_p = jnp.maximum(load_p, turn(load_p, -1))
        worst_p = jnp.maximum(worst_p, turn(worst_p, -2))
        worst_m = jnp.maximum(load_m, turn(load_m, 1))
        worst_m = jnp.maximum(worst_m, turn(worst_m, 2))
        share = jnp.minimum(jnp.maximum((across + worst_m - worst_p + 1) >> 1, 0), across)
        chosen = (sub & 3) == phase
        share_p = jnp.where(chosen, share, 0)
        share_m = jnp.where(chosen, across - share, 0)
        forward = forward + share_p
        share_p = share_p + turn(share_p, 1)
        load_p = load_p + share_p + turn(share_p, 2)
        share_m = share_m + turn(share_m, -1)
        load_m = load_m + share_m + turn(share_m, -2)
    opposite = tall(jnp.where(ahead == 4, src, 8))
    nth = over_all(jnp.where(jnp.logical_and(jnp.transpose(opposite) == opposite, low < line), 1, 0))
    quota = over_all(jnp.where(src == sub, forward, 0))
    plus = jnp.logical_and(ahead > 0, jnp.logical_or(ahead < 4, jnp.logical_and(ahead == 4, nth < quota)))
    minus = jnp.logical_or(ahead > 4, jnp.logical_and(ahead == 4, nth >= quota))
    dist = jnp.where(plus, ahead, jnp.where(minus, 8 - ahead, 0))
    group = jnp.where(ahead > 0, src * 2 + jnp.where(minus, 1, 0), 16)
    order = group * 1024 + (4 - dist) * 128 + lane
    wide = tall(order)
    if shared is None:
        active = lane >= 0
    else:
        packed = tall(shared * 32768 + order)
        column = jnp.transpose(packed)
        same = (packed >> 10) == (column >> 10)
        active = over_all(jnp.where(jnp.logical_and(same, column < packed), 1, 0)) == 0
    column = jnp.transpose(tall(jnp.where(active, order, 32767)))
    rank = over_all(jnp.where(jnp.logical_and((column >> 10) == (wide >> 10), column < wide), 1, 0))
    if shared is not None:
        led = jnp.transpose(tall(jnp.where(active, rank, 0)))
        rank = over_all(jnp.where(same, led, 0))
    result = []
    longest = jnp.zeros((8, 128), jnp.int32)
    for sign, act in ((1, plus), (-1, minus)):
        goes = jnp.logical_and(act, active)
        counts = [per_chip(jnp.logical_and(goes, dist > h)) for h in range(4)]
        starts = [jnp.zeros((8, 128), jnp.int32)]
        for h in range(1, 4):
            starts.append(
                jnp.maximum(
                    starts[h - 1] + turn(counts[h - 1], sign * (h - 1)),
                    turn(starts[h - 1], sign) + LAG,
                )
            )
        for h in range(4):
            here = turn(counts[h], sign * h)
            longest = jnp.maximum(longest, jnp.where(here > 0, starts[h] + here, 0))
        age = (sign * (chip - src)) & 7
        out_start = jnp.zeros((8, 128), jnp.int32)
        in_start = jnp.zeros((8, 128), jnp.int32)
        before_chip = (chip - sign) & 7
        for h in range(4):
            out_start = jnp.where(age == h, pick_row(starts[h], sub, chip), out_start)
            in_start = jnp.where(age == h + 1, pick_row(starts[h], sub, before_chip), in_start)
        leaves = jnp.logical_and(goes, age < dist)
        arrives = jnp.logical_and(act, age == dist)
        out_slot = out_start + rank
        in_slot = in_start + rank
        source = jnp.where(age == 0, own_index + 1, 65 + in_slot)
        result.append((leaves, out_slot, source, arrives, in_slot))
    return result, bcast(jnp.max(longest, axis=0, keepdims=True))


def by_row(mask, place, value, rows):
    reps = rows // 8
    wide = [jnp.concatenate([v] * reps, axis=0) for v in (jnp.where(mask, place, -1), value)]
    sub = lax.broadcasted_iota(jnp.int32, (rows, 128), 0)
    return jnp.sum(jnp.where(wide[0] == sub, wide[1], 0), axis=1, keepdims=True)


def make_tables(ids, me):
    chip = me // 2
    sub = lax.broadcasted_iota(jnp.int32, (8, 128), 0)
    lane = lax.broadcasted_iota(jnp.int32, (8, 128), 1)
    token_chip = lane >> 4
    owner_chip = ids >> 6
    chip_slot = ids & 63
    mine = (ids >> 5) == me
    fetch, longest_f = slot_plan(owner_chip, token_chip, chip_slot, ids, chip, sub, lane)
    back, longest_b = slot_plan(token_chip, owner_chip, lane & 15, None, chip, sub, lane)
    fits = jnp.logical_and(longest_f <= SLOTS_OUT, longest_b <= SLOTS_BACK)
    columns = []
    for plan in (fetch, back):
        for leaves, out_slot, source, _, _ in plan:
            columns.append(by_row(leaves, out_slot, source, 32))
    where = jnp.where(owner_chip == token_chip, chip_slot + 1, 0)
    for d in range(2):
        where = jnp.where(fetch[d][3], 65 + d * SLOTS_OUT + fetch[d][4], where)
    columns.append(by_row((lane >> 3) == me, lane & 7, where, 32))
    stays = jnp.logical_and(owner_chip == token_chip, token_chip == chip)
    landing = jnp.where(stays, 2 * SLOTS_BACK + (lane & 15), -1)
    for d in range(2):
        landing = jnp.where(back[d][3], d * SLOTS_BACK + back[d][4], landing)
    wanted = jnp.logical_and(landing >= 0, mine)
    count = bcast(jnp.sum(jnp.where(wanted, 1, 0), axis=1, keepdims=True))
    line = lax.broadcasted_iota(jnp.int32, (128, 128), 1)
    ahead = jnp.transpose(jnp.concatenate([jnp.where(wanted, lane, 128)] * 16, axis=0))
    rank = bcast(jnp.sum(jnp.where(ahead < line, 1, 0), axis=0, keepdims=True))
    entry = jnp.where(wanted, rank * 4096 + landing * 32 + (ids & 31), -1)
    entry = jnp.transpose(jnp.concatenate([entry] * 16, axis=0))
    listed = bcast(jnp.sum(jnp.where((entry >> 12) == line, entry & 4095, 0), axis=0, keepdims=True))
    wide_lane = lax.broadcasted_iota(jnp.int32, (32, 128), 1)
    table = jnp.concatenate([jnp.where(fits, 1, 0)] * 4, axis=0)
    for i, column in enumerate(columns):
        table = jnp.where(wide_lane == i, jnp.broadcast_to(column, (32, 128)), table)
    return jnp.concatenate([table, jnp.where(sub == 0, listed, count)], axis=0)


def wait_bytes(ref, sem):
    pltpu.make_async_copy(ref, ref, sem).wait()


def ring_kernel(hw, dw, ids_ref, hid_hbm, og_hbm, a_hbm, b_hbm, table_ref, fac_a, back_ref, fin_a, fin_b,
                idbuf, table, fac_b, proj_ref, hid, og, grads_a, grads_b,
                own_ra, own_rb, own_sa, own_sb, picked_a, picked_b, items_a, items_b,
                stage_fa, stage_fb, stage_ra, stage_rb, got_fa, got_fb, got_ra, got_rb, kept_a, kept_b,
                part, parts, sums, loc, ids_sem, sib, swap_sem, ring_send, ring_recv, fwd, psum_sem):
    me = lax.axis_index("dp")
    t = lax.axis_index("tensor")
    chip = me // 2
    core = me % 2
    other = 1 - core
    sibling = {"dp": chip * 2 + other}
    mine32 = pl.ds(pl.multiple_of(core * OWNED, OWNED), OWNED)
    mine8 = pl.ds(pl.multiple_of(core * NBLK, NBLK), NBLK)

    def far(src, dst, send, recv, where):
        return pltpu.make_async_remote_copy(
            src_ref=src, dst_ref=dst, send_sem=send, recv_sem=recv, device_id=where, device_id_type=MESH
        )

    def lanes(width, which):
        return pl.ds(pl.multiple_of(which * width, 128), width)

    def cut(ref, width, which):
        return ref.at[:, :, lanes(width, which)]

    barrier = pltpu.get_barrier_semaphore()
    for o in range(1, NDP):
        pl.semaphore_signal(barrier, inc=1, device_id={"dp": lax.rem(me + o, NDP)}, device_id_type=MESH)
    for o in range(1, NT):
        pl.semaphore_signal(barrier, inc=1, device_id={"tensor": lax.rem(t + o, NT)}, device_id_type=MESH)
    owns = ((b_hbm, own_rb, dw, core), (a_hbm, own_ra, hw, core), (b_hbm, own_sb, dw, other), (a_hbm, own_sa, hw, other))
    for i, (ref, dst, width, which) in enumerate(owns):
        pltpu.make_async_copy(cut(ref, width, which), dst.at[mine32], loc.at[i]).start()
    pltpu.make_async_copy(og_hbm, og, loc.at[4]).start()
    pltpu.make_async_copy(hid_hbm, hid, loc.at[5]).start()

    lane = lax.broadcasted_iota(jnp.int32, (8, 128), 1)
    mine_ids = jnp.zeros((8, 128), jnp.int32)
    for j in range(NBLK):
        mine_ids = jnp.where(lane == me * NBLK + j, ids_ref[j], mine_ids)
    idbuf[me] = mine_ids
    pl.semaphore_wait(barrier, NDP - 1 + NT - 1)

    for o in range(1, NDP):
        far(idbuf.at[me], idbuf.at[me], ids_sem.at[0], ids_sem.at[1], {"dp": lax.rem(me + o, NDP)}).start()
    for i, (ref, dst, width, which) in enumerate(owns):
        far(cut(ref, width, 1 - which), dst.at[mine32], sib.at[0, i], sib.at[1, i], sibling).start()

    def own_ready(i):
        dst = owns[i][1].at[pl.ds(0, OWNED)]
        wait_bytes(dst, loc.at[i])
        wait_bytes(dst, sib.at[1, i])

    wait_bytes(idbuf.at[pl.ds(0, NDP - 1)], ids_sem.at[1])
    ids = idbuf[0]
    for i in range(1, NDP):
        ids = ids + idbuf[i]
    table_ref[...] = make_tables(ids, me)
    to_smem = pltpu.make_async_copy(table_ref, table, loc.at[6])
    to_smem.start()
    to_smem.wait()

    def stream(index, phase, own, stage, got, kept, land_at, keep_local, group):
        count = own.shape[0]
        slots = stage.shape[1]
        behind = LAG // group
        chunks = [(p, min(group, slots - p)) for p in range(0, slots, group)]
        everything = kept.at[pl.ds(0, 2 * slots)]

        def copy(d, q):
            p, n = chunks[q]
            return far(
                stage.at[d, pl.ds(p, n)],
                got.at[d, pl.ds(p, n)],
                ring_send.at[index],
                ring_recv.at[index, d, q],
                {"dp": lax.rem(chip + (1 if d == 0 else NCHIP - 1), NCHIP) * 2 + core},
            )

        def landed(d, q):
            copy(d, q).wait_recv()
            p, n = chunks[q]
            there = land_at(pl.ds(d * slots + p, n))
            far(got.at[d, pl.ds(p, n)], there, fwd.at[index, 1], fwd.at[index, 2], sibling).start()
            if keep_local:
                pltpu.make_async_copy(got.at[d, pl.ds(p, n)], there, fwd.at[index, 0]).start()
            kept[pl.ds(d * slots + p, n)] = got[d, pl.ds(p, n)]

        def step(m):
            for d in range(2):
                if m >= behind:
                    landed(d, m - behind)
                if m < len(chunks):
                    p, n = chunks[m]
                    for i in range(n):
                        code = table[p + i, phase * 2 + d]
                        value = own[jnp.clip(code - 1, 0, count - 1)]
                        if m >= behind:
                            passed = kept[d * slots + jnp.clip(code - 65, 0, slots - 1)]
                            value = jnp.where(code > 64, passed, value)
                        stage[d, p + i] = value
                    copy(d, m).start()

        def arrived():
            if keep_local:
                wait_bytes(everything, fwd.at[index, 0])
            wait_bytes(everything, fwd.at[index, 2])

        def finish():
            wait_bytes(stage, ring_send.at[index])
            wait_bytes(everything, fwd.at[index, 1])

        return step, arrived, finish

    def play(order, a, b, **others):
        step = {"a": 0, "b": 0}
        for kind in order:
            if kind in others:
                others[kind]()
            else:
                (a if kind == "a" else b)(step[kind])
                step[kind] += 1

    fa, fa_arrived, fa_finish = stream(
        0, 0, own_ra, stage_fa, got_fa, kept_a, lambda s: picked_a.at[s], False, 2
    )
    fb, fb_arrived, fb_finish = stream(
        1, 0, own_rb, stage_fb, got_fb, kept_b, lambda s: picked_b.at[s], False, 2
    )
    ra, ra_arrived, ra_finish = stream(
        2, 1, items_a, stage_ra, got_ra, kept_a, lambda s: fin_a.at[s, :, lanes(hw, core)], True, 2
    )
    rb, rb_arrived, rb_finish = stream(
        3, 1, items_b, stage_rb, got_rb, kept_b, lambda s: fin_b.at[s, :, lanes(dw, core)], True, 2
    )

    def choose(j, fac, own_r, own_s, kept, picked, width):
        code = table[j, 4]
        near = code <= 64
        at = jnp.clip(code - 1, 0, 2 * OWNED - 1)
        away = jnp.clip(code - 65, 0, 2 * SLOTS_OUT - 1)
        fac[j, :, lanes(width, core)] = jnp.where(near, own_r[at], kept[away])
        fac[j, :, lanes(width, other)] = jnp.where(near, own_s[at], picked[away])

    def project(i, fac, rows_ref):
        for j in range(NBLK):
            term = lax.dot_general(
                fac[j], rows_ref[pl.ds(j * BLOCK, BLOCK)], (((1,), (1,)), ((), ())),
                preferred_element_type=jnp.float32,
            )
            part[i, 2 * j] = term[:8]
            part[i, 2 * j + 1] = term[8:]

    def peers():
        return [lax.rem(t + o, NT) for o in range(1, NT)]

    def scatter(i):
        parts[i, t] = part[i, t]
        for peer in peers():
            far(part.at[i, peer], parts.at[i, t], psum_sem.at[i, 0], psum_sem.at[i, 1], {"tensor": peer}).start()

    def reduce(i):
        wait_bytes(parts.at[i, pl.ds(0, NT - 1)], psum_sem.at[i, 1])
        total = parts[i, 0]
        for n in range(1, NT):
            total = total + parts[i, n]
        sums[i, t] = total
        for peer in peers():
            far(sums.at[i, t], sums.at[i, t], psum_sem.at[i, 2], psum_sem.at[i, 3], {"tensor": peer}).start()

    def gather(i, out):
        wait_bytes(sums.at[i, pl.ds(0, NT - 1)], psum_sem.at[i, 3])
        for j in range(NBLK):
            out[j] = jnp.concatenate([sums[i, 2 * j], sums[i, 2 * j + 1]], axis=0).astype(jnp.bfloat16)

    def gradient(low, rows_ref, grads, width, which):
        for j in range(NBLK):
            grad = adapter_scale * jnp.dot(
                low[j], rows_ref[pl.ds(j * BLOCK, BLOCK), lanes(width, which)], preferred_element_type=jnp.float32
            )
            grads[j, :, lanes(width, which)] = grad.astype(jnp.bfloat16)

    tail8 = pl.ds(2 * SLOTS_BACK + core * NBLK, NBLK)

    def hand_over(i, low, rows_ref, grads, items, fin, width):
        gradient(low, rows_ref, grads, width, other)
        swap = far(cut(grads, width, other), items.at[mine8], swap_sem.at[i, 0], swap_sem.at[i, 1], sibling)
        swap.start()
        gradient(low, rows_ref, grads, width, core)
        items[mine8] = grads[:, :, lanes(width, core)]
        share = far(grads, fin.at[tail8], swap_sem.at[i, 2], swap_sem.at[i, 3], sibling)
        share.start()
        keep = pltpu.make_async_copy(grads, fin.at[tail8], swap_sem.at[i, 4])
        keep.start()
        return swap, share, keep

    def back_part():
        own_ready(2)
        fb_arrived()
        wait_bytes(og, loc.at[4])
        for j in range(NBLK):
            choose(j, fac_b, own_rb, own_sb, kept_b, picked_b, dw)
        project(0, fac_b, og)
        scatter(0)

    own_ready(0)
    own_ready(1)
    play(ORDER_OUT, fa, fb, P=back_part, R=lambda: reduce(0))
    own_ready(3)
    fa_arrived()
    wait_bytes(hid, loc.at[5])
    for j in range(NBLK):
        choose(j, fac_a, own_ra, own_sa, kept_a, picked_a, hw)
    project(1, fac_a, hid)
    scatter(1)
    gather(0, back_ref)
    moves_a = hand_over(0, back_ref, hid, grads_a, items_a, fin_a, hw)
    moves_a[0].wait_recv()
    moves_b = []

    def proj_part():
        gather(1, proj_ref)
        moves_b.extend(hand_over(1, proj_ref, og, grads_b, items_b, fin_b, dw))

    play(ORDER_BACK, ra, rb, S=lambda: reduce(1), G=proj_part, X=lambda: moves_b[0].wait_recv())

    ra_arrived()
    rb_arrived()
    for swap, share, keep in (moves_a, moves_b):
        swap.wait_send()
        share.wait()
        keep.wait()
    wait_bytes(idbuf.at[pl.ds(0, NDP - 1)], ids_sem.at[0])
    for i in range(4):
        wait_bytes(owns[i][1].at[pl.ds(0, OWNED)], sib.at[0, i])
    for i in range(2):
        wait_bytes(parts.at[i, pl.ds(0, NT - 1)], psum_sem.at[i, 0])
        wait_bytes(sums.at[i, pl.ds(0, NT - 1)], psum_sem.at[i, 2])
    fa_finish()
    fb_finish()
    ra_finish()
    rb_finish()


def last_kernel(table, fin_a, fin_b, fac, back, gh, ga, gb, acc_a, acc_b, buf_a, buf_b, ghb, gab, gbb, sems):
    count = table[33, 0]

    def arriving(p):
        slot = table[32, p] >> 5
        return (
            pltpu.make_async_copy(fin_a.at[slot], buf_a.at[p], sems.at[0]),
            pltpu.make_async_copy(fin_b.at[slot], buf_b.at[p], sems.at[4]),
        )

    def loop(step):
        def run(p, carry):
            step(p)
            return carry

        lax.fori_loop(0, count, run, 0)

    def start(p):
        for copy in arriving(p):
            copy.start()

    def wait(p):
        for copy in arriving(p):
            copy.wait()

    loop(start)
    for j in range(NBLK):
        rows = pl.ds(j * BLOCK, BLOCK)
        rows_out = adapter_scale * lax.dot_general(
            back[j], fac[j], (((0,), (0,)), ((), ())), preferred_element_type=jnp.float32
        )
        ghb[rows] = rows_out.astype(jnp.bfloat16)
        pltpu.make_async_copy(ghb.at[rows], gh.at[rows], sems.at[1]).start()
    gab[...] = jnp.zeros_like(gab)
    gbb[...] = jnp.zeros_like(gbb)
    trio = ((acc_a, buf_a, gab), (acc_b, buf_b, gbb))

    def clear(p):
        for acc, _, _ in trio:
            acc[table[32, p] & 31] = jnp.zeros(acc.shape[1:], jnp.float32)

    def add(p):
        for acc, buf, _ in trio:
            acc[table[32, p] & 31] += buf[p].astype(jnp.float32)

    def store(p):
        for acc, _, out in trio:
            out[table[32, p] & 31] = acc[table[32, p] & 31].astype(jnp.bfloat16)

    loop(clear)
    loop(wait)
    loop(add)
    loop(store)
    ca = pltpu.make_async_copy(gab, ga, sems.at[2])
    cb = pltpu.make_async_copy(gbb, gb, sems.at[3])
    ca.start()
    cb.start()
    pltpu.make_async_copy(ghb, gh, sems.at[1]).wait()
    ca.wait()
    cb.wait()


def shards(hidden, output_gradient, block_adapter_index, adapter_down_factors, adapter_up_factors):
    rows, ff_local = hidden.shape
    d_local = output_gradient.shape[1]
    hw, dw = ff_local // 2, d_local // 2
    bf16, f32 = jnp.bfloat16, jnp.float32
    vmem = pl.BlockSpec(memory_space=pltpu.VMEM)
    smem = pl.BlockSpec(memory_space=pltpu.SMEM)
    anywhere = pl.BlockSpec(memory_space=pl.ANY)
    dma = pltpu.SemaphoreType.DMA
    rank = ADAPTER_RANK
    streams = [
        pltpu.VMEM((2, slots, rank, width), bf16) for slots in (SLOTS_OUT, SLOTS_BACK) for width in (hw, dw)
    ]
    scratch = [
        pltpu.VMEM((NDP, 8, 128), jnp.int32),
        pltpu.SMEM((40, 128), jnp.int32),
        pltpu.VMEM((NBLK, rank, d_local), bf16),
        pltpu.VMEM((NBLK, rank, BLOCK), bf16),
        pltpu.VMEM((rows, ff_local), bf16),
        pltpu.VMEM((rows, d_local), bf16),
        pltpu.VMEM((NBLK, rank, ff_local), bf16),
        pltpu.VMEM((NBLK, rank, d_local), bf16),
        pltpu.VMEM((2 * OWNED, rank, hw), bf16),
        pltpu.VMEM((2 * OWNED, rank, dw), bf16),
        pltpu.VMEM((2 * OWNED, rank, hw), bf16),
        pltpu.VMEM((2 * OWNED, rank, dw), bf16),
        pltpu.VMEM((2 * SLOTS_OUT, rank, hw), bf16),
        pltpu.VMEM((2 * SLOTS_OUT, rank, dw), bf16),
        pltpu.VMEM((2 * NBLK, rank, hw), bf16),
        pltpu.VMEM((2 * NBLK, rank, dw), bf16),
        *streams,
        *streams,
        pltpu.VMEM((2 * SLOTS_BACK, rank, hw), bf16),
        pltpu.VMEM((2 * SLOTS_BACK, rank, dw), bf16),
        pltpu.VMEM((2, NT, 8, BLOCK), f32),
        pltpu.VMEM((2, NT, 8, BLOCK), f32),
        pltpu.VMEM((2, NT, 8, BLOCK), f32),
        dma((7,)),
        dma((2,)),
        dma((2, 4)),
        dma((2, 5)),
        dma((4,)),
        dma((4, 2, max(SLOTS_OUT, SLOTS_BACK))),
        dma((4, 3)),
        dma((2, 4)),
    ]
    table, fac, back, fin_a, fin_b = pl.pallas_call(
        functools.partial(ring_kernel, hw, dw),
        name="ring",
        out_shape=(
            jax.ShapeDtypeStruct((40, 128), jnp.int32),
            jax.ShapeDtypeStruct((NBLK, rank, ff_local), bf16),
            jax.ShapeDtypeStruct((NBLK, rank, BLOCK), bf16),
            jax.ShapeDtypeStruct((NFIN, rank, ff_local), bf16),
            jax.ShapeDtypeStruct((NFIN, rank, d_local), bf16),
        ),
        in_specs=[smem] + [anywhere] * 4,
        out_specs=(vmem, vmem, vmem, anywhere, anywhere),
        scratch_shapes=scratch,
        compiler_params=pltpu.CompilerParams(
            collective_id=0, has_side_effects=True, vmem_limit_bytes=VMEM_LIMIT
        ),
    )(block_adapter_index, hidden, output_gradient, adapter_down_factors, adapter_up_factors)

    def finish(*_):
        return pl.pallas_call(
            last_kernel,
            name="finish",
            out_shape=(
                jax.ShapeDtypeStruct((rows, ff_local), bf16),
                jax.ShapeDtypeStruct(adapter_down_factors.shape, bf16),
                jax.ShapeDtypeStruct(adapter_up_factors.shape, bf16),
            ),
            in_specs=[smem, anywhere, anywhere, vmem, vmem],
            out_specs=(anywhere, anywhere, anywhere),
            scratch_shapes=[
                pltpu.VMEM((OWNED, rank, ff_local), f32),
                pltpu.VMEM((OWNED, rank, d_local), f32),
                pltpu.VMEM((NFIN, rank, ff_local), bf16),
                pltpu.VMEM((NFIN, rank, d_local), bf16),
                pltpu.VMEM((rows, ff_local), bf16),
                pltpu.VMEM((OWNED, rank, ff_local), bf16),
                pltpu.VMEM((OWNED, rank, d_local), bf16),
                dma((5,)),
            ],
            compiler_params=pltpu.CompilerParams(vmem_limit_bytes=VMEM_LIMIT),
        )(table, fin_a, fin_b, fac, back)

    return lax.cond(
        table[0, 8] > 0,
        finish,
        general,
        hidden,
        output_gradient,
        block_adapter_index,
        adapter_down_factors,
        adapter_up_factors,
    )


def solution(mesh):
    placed = (
        P("dp", "tensor"),
        P("dp", "tensor"),
        P("dp"),
        P("dp", None, "tensor"),
        P("dp", None, "tensor"),
    )
    return jax.shard_map(
        shards,
        mesh=mesh,
        in_specs=placed,
        out_specs=(P("dp", "tensor"), P("dp", None, "tensor"), P("dp", None, "tensor")),
        check_vma=False,
    )
```

```python
import functools

import jax
import jax.numpy as jnp
from jax import lax
from jax.experimental import pallas as pl
from jax.experimental.pallas import tpu as pltpu
from jax.sharding import PartitionSpec as P

ADAPTER_RANK = 16
BLOCK = 128
CAP = 2
MESH = pl.DeviceIdType.MESH
NDP = 16
NCHIP = 8
NT = 16
NBLK = 8
OWNED = 32
SLOTS_OUT = 25
SLOTS_BACK = 26
LAG = 6
TWO_FIRST, TWO = 8, 13
ONE_FIRST, ONE = 3, 10
EXPRESS = TWO + ONE
NFIN = 2 * max(SLOTS_BACK, EXPRESS) + 16
FLAG = 12
ORDER = "baabaaabaPaaaaRaaaHaaaWAAQAAAASAAAAGAXBAAABAAB"
VMEM_LIMIT = 56 * 1024 * 1024


adapter_scale = 2.0


def general(hidden, output_gradient, block_adapter_index, adapter_down_factors, adapter_up_factors):
    dp_size = lax.axis_size("dp")
    my_index = lax.axis_index("dp")
    block_count = block_adapter_index.shape[0]
    owned_adapter_count = adapter_down_factors.shape[0]
    ff_local = hidden.shape[1]
    d_local = output_gradient.shape[1]
    slot_count = dp_size * CAP
    all_ids = lax.all_gather(block_adapter_index, "dp", axis=0, tiled=True).reshape(
        dp_size, block_count
    )
    owners = all_ids // owned_adapter_count
    local_ids = all_ids % owned_adapter_count
    same_owner = owners[:, :, None] == owners[:, None, :]
    block_range = jnp.arange(block_count, dtype=jnp.int32)
    earlier = block_range[None, :] < block_range[:, None]
    rank_in = jnp.sum(jnp.logical_and(same_owner, earlier[None, :, :]), axis=2)
    cap_range = jnp.arange(CAP, dtype=jnp.int32)
    chosen = jnp.logical_and(
        (owners == my_index)[:, None, :], rank_in[:, None, :] == cap_range[None, :, None]
    )
    owned_range = jnp.arange(owned_adapter_count, dtype=jnp.int32)
    local_match = local_ids[:, :, None] == owned_range[None, None, :]
    selection_table = jnp.sum(
        jnp.logical_and(chosen[:, :, :, None], local_match[:, None, :, :]), axis=2
    )
    selection_table = selection_table.reshape(slot_count, owned_adapter_count).astype(jnp.bfloat16)
    send_a = jnp.einsum(
        "dz,zeg->deg", selection_table, adapter_down_factors, preferred_element_type=jnp.float32
    ).astype(jnp.bfloat16)
    send_b = jnp.einsum(
        "ge,elq->glq", selection_table, adapter_up_factors, preferred_element_type=jnp.float32
    ).astype(jnp.bfloat16)
    send_a = send_a.reshape(dp_size, CAP, ADAPTER_RANK, ff_local)
    send_b = send_b.reshape(dp_size, CAP, ADAPTER_RANK, d_local)
    fetched_a, fetched_b = (
        lax.all_to_all(send_a, "dp", split_axis=0, concat_axis=0, tiled=True),
        lax.all_to_all(send_b, "dp", split_axis=0, concat_axis=0, tiled=True),
    )
    fetched_a = fetched_a.reshape(slot_count, ADAPTER_RANK, ff_local)
    fetched_b = fetched_b.reshape(slot_count, ADAPTER_RANK, d_local)
    my_owners = jnp.take(owners, my_index, axis=0)
    my_ranks = jnp.take(rank_in, my_index, axis=0)
    my_slots = my_owners * CAP + my_ranks
    down_factor = jnp.take(fetched_a, my_slots, axis=0)
    up_factor = jnp.take(fetched_b, my_slots, axis=0)
    hid_blocks = hidden.reshape(block_count, BLOCK, ff_local)
    out_blocks = output_gradient.reshape(block_count, BLOCK, d_local)
    proj_part = jnp.einsum(
        "jtf,jrf->jtr", hid_blocks, down_factor, preferred_element_type=jnp.float32
    )
    back_part = jnp.einsum(
        "jtd,jrd->jtr", out_blocks, up_factor, preferred_element_type=jnp.float32
    )
    proj, back = lax.psum((proj_part, back_part), "tensor")
    projected_up = proj.astype(jnp.bfloat16)
    backward_up = back.astype(jnp.bfloat16)
    block_down_gradient = (
        adapter_scale
        * jnp.einsum("jtr,jtf->jrf", backward_up, hid_blocks, preferred_element_type=jnp.float32)
    ).astype(jnp.bfloat16)
    block_up_gradient = (
        adapter_scale
        * jnp.einsum("jtr,jtd->jrd", projected_up, out_blocks, preferred_element_type=jnp.float32)
    ).astype(jnp.bfloat16)
    gradient_rows = adapter_scale * jnp.einsum(
        "jtr,jrf->jtf", backward_up, down_factor, preferred_element_type=jnp.float32
    )
    grad_hidden = gradient_rows.astype(jnp.bfloat16).reshape(block_count * BLOCK, ff_local)
    slot_range = jnp.arange(slot_count, dtype=jnp.int32)
    place_table = (slot_range[:, None] == my_slots[None, :]).astype(jnp.bfloat16)
    back_a = jnp.einsum(
        "kj,jrf->krf", place_table, block_down_gradient, preferred_element_type=jnp.float32
    ).astype(jnp.bfloat16)
    back_bb = jnp.einsum(
        "kj,jrd->krd", place_table, block_up_gradient, preferred_element_type=jnp.float32
    ).astype(jnp.bfloat16)
    back_a = back_a.reshape(dp_size, CAP, ADAPTER_RANK, ff_local)
    back_bb = back_bb.reshape(dp_size, CAP, ADAPTER_RANK, d_local)
    recv_a, recv_b = (
        lax.all_to_all(back_a, "dp", split_axis=0, concat_axis=0, tiled=True),
        lax.all_to_all(back_bb, "dp", split_axis=0, concat_axis=0, tiled=True),
    )
    sum_table = jnp.transpose(selection_table)
    grad_a = jnp.einsum(
        "ak,krf->arf",
        sum_table,
        recv_a.reshape(slot_count, ADAPTER_RANK, ff_local),
        preferred_element_type=jnp.float32,
    )
    grad_b = jnp.einsum(
        "ak,krd->ard",
        sum_table,
        recv_b.reshape(slot_count, ADAPTER_RANK, d_local),
        preferred_element_type=jnp.float32,
    )
    return (grad_hidden, grad_a.astype(jnp.bfloat16), grad_b.astype(jnp.bfloat16))


def bcast(x, shape=(8, 128)):
    return jnp.broadcast_to(x, shape)


def pick_row(x, sub, row):
    return bcast(jnp.sum(jnp.where(sub == row, x, 0), axis=0, keepdims=True))


def turn(x, by):
    by = by % 8
    return pltpu.roll(x, by, 0) if by else x


def tall(x):
    return jnp.concatenate([x] * 16, axis=0)


def slot_plan(src, dst, own_index, shared, chip, sub, lane):
    ahead = (dst - src) & 7
    low = lax.broadcasted_iota(jnp.int32, (128, 128), 0)
    line = lax.broadcasted_iota(jnp.int32, (128, 128), 1)

    def per_chip(mask):
        return bcast(jnp.sum(jnp.where(jnp.logical_and(src == sub, mask), 1, 0), axis=1, keepdims=True))

    def over_all(x):
        return bcast(jnp.sum(x, axis=0, keepdims=True))

    one, two, three, across, five, six, seven = [per_chip(ahead == d) for d in range(1, 8)]
    load_p = one + two + three + turn(two + three, 1) + turn(three, 2)
    load_m = seven + six + five + turn(six + five, -1) + turn(five, -2)
    forward = jnp.zeros((8, 128), jnp.int32)
    for phase in range(4):
        worst_p = jnp.maximum(load_p, turn(load_p, -1))
        worst_p = jnp.maximum(worst_p, turn(worst_p, -2))
        worst_m = jnp.maximum(load_m, turn(load_m, 1))
        worst_m = jnp.maximum(worst_m, turn(worst_m, 2))
        share = jnp.minimum(jnp.maximum((across + worst_m - worst_p + 1) >> 1, 0), across)
        chosen = (sub & 3) == phase
        share_p = jnp.where(chosen, share, 0)
        share_m = jnp.where(chosen, across - share, 0)
        forward = forward + share_p
        share_p = share_p + turn(share_p, 1)
        load_p = load_p + share_p + turn(share_p, 2)
        share_m = share_m + turn(share_m, -1)
        load_m = load_m + share_m + turn(share_m, -2)
    opposite = tall(jnp.where(ahead == 4, src, 8))
    nth = over_all(jnp.where(jnp.logical_and(jnp.transpose(opposite) == opposite, low < line), 1, 0))
    quota = over_all(jnp.where(src == sub, forward, 0))
    plus = jnp.logical_and(ahead > 0, jnp.logical_or(ahead < 4, jnp.logical_and(ahead == 4, nth < quota)))
    minus = jnp.logical_or(ahead > 4, jnp.logical_and(ahead == 4, nth >= quota))
    dist = jnp.where(plus, ahead, jnp.where(minus, 8 - ahead, 0))
    group = jnp.where(ahead > 0, src * 2 + jnp.where(minus, 1, 0), 16)
    order = group * 1024 + (4 - dist) * 128 + lane
    wide = tall(order)

    def ranked(active):
        column = jnp.transpose(tall(jnp.where(active, order, 32767)))
        return over_all(jnp.where(jnp.logical_and((column >> 10) == (wide >> 10), column < wide), 1, 0))

    everyone = lane >= 0
    plain_rank = ranked(everyone)
    if shared is None:
        active, rank = everyone, plain_rank
    else:
        packed = tall(shared * 32768 + order)
        column = jnp.transpose(packed)
        same = (packed >> 10) == (column >> 10)
        active = over_all(jnp.where(jnp.logical_and(same, column < packed), 1, 0)) == 0
        led = jnp.transpose(tall(jnp.where(active, ranked(active), 0)))
        rank = over_all(jnp.where(same, led, 0))
    hops = []
    express = []
    longest = jnp.zeros((8, 128), jnp.int32)
    crowded = jnp.zeros((8, 128), jnp.int32)
    for sign, act in ((1, plus), (-1, minus)):
        age = (sign * (chip - src)) & 7
        arrives = jnp.logical_and(act, age == dist)
        goes = jnp.logical_and(act, active)
        counts = [per_chip(jnp.logical_and(goes, dist > h)) for h in range(4)]
        starts = [jnp.zeros((8, 128), jnp.int32)]
        for h in range(1, 4):
            starts.append(
                jnp.maximum(
                    starts[h - 1] + turn(counts[h - 1], sign * (h - 1)),
                    turn(starts[h - 1], sign) + LAG,
                )
            )
        for h in range(4):
            here = turn(counts[h], sign * h)
            longest = jnp.maximum(longest, jnp.where(here > 0, starts[h] + here, 0))
        out_start = jnp.zeros((8, 128), jnp.int32)
        in_start = jnp.zeros((8, 128), jnp.int32)
        before_chip = (chip - sign) & 7
        for h in range(4):
            out_start = jnp.where(age == h, pick_row(starts[h], sub, chip), out_start)
            in_start = jnp.where(age == h + 1, pick_row(starts[h], sub, before_chip), in_start)
        leaves = jnp.logical_and(goes, age < dist)
        in_slot = in_start + rank
        source = jnp.where(age == 0, own_index + 1, 65 + in_slot)
        hops.append((leaves, out_start + rank, source, arrives, in_slot))

        if shared is not None:
            counts = [per_chip(jnp.logical_and(act, dist > h)) for h in range(4)]
        single, third = counts[0] - counts[1], counts[2] - counts[3]
        two_start = jnp.maximum(counts[1], TWO_FIRST)
        one_start = jnp.maximum(single, ONE_FIRST)
        passing4 = turn(counts[3], 2 * sign)
        passing3 = turn(third, 2 * sign)
        two_end = jnp.where(passing4 > 0, two_start + passing4, counts[1])
        one_end = jnp.where(passing3 > 0, one_start + passing3, single)
        full = jnp.logical_or(
            jnp.logical_or(two_end > TWO, one_end > ONE), counts[2] > TWO_FIRST
        )
        crowded = jnp.maximum(crowded, jnp.where(full, 1, 0))
        far_before = over_all(jnp.where(src == sub, counts[1], 0))
        four_before = over_all(jnp.where(src == sub, counts[3], 0))
        own = age == 0
        passes = age == 2
        as_two = jnp.logical_and(own, dist >= 2)
        as_one = jnp.logical_and(own, dist == 1)
        on_two = jnp.logical_and(passes, dist == 4)
        on_one = jnp.logical_and(passes, dist == 3)
        leaves = jnp.logical_and(
            act, jnp.logical_or(jnp.logical_or(as_two, as_one), jnp.logical_or(on_two, on_one))
        )
        near_slot = TWO + plain_rank - far_before
        third_slot = TWO + plain_rank - four_before
        out_slot = jnp.where(as_one, near_slot, plain_rank)
        out_slot = jnp.where(on_two, pick_row(two_start, sub, chip) + plain_rank, out_slot)
        out_slot = jnp.where(on_one, pick_row(one_start, sub, chip) + third_slot, out_slot)
        source = jnp.where(own, own_index + 1, 65 + plain_rank)
        in_slot = jnp.where(dist == 1, near_slot, plain_rank)
        in_slot = jnp.where(dist == 3, pick_row(one_start, sub, before_chip) + third_slot, in_slot)
        in_slot = jnp.where(
            dist == 4, pick_row(two_start, sub, (chip - 2 * sign) & 7) + plain_rank, in_slot
        )
        express.append((leaves, out_slot, source, arrives, in_slot))
    return hops, express, bcast(jnp.max(longest, axis=0, keepdims=True)), over_all(crowded)


def by_row(mask, place, value, rows):
    reps = rows // 8
    wide = [jnp.concatenate([v] * reps, axis=0) for v in (jnp.where(mask, place, -1), value)]
    sub = lax.broadcasted_iota(jnp.int32, (rows, 128), 0)
    return jnp.sum(jnp.where(wide[0] == sub, wide[1], 0), axis=1, keepdims=True)


def make_tables(ids, me):
    chip = me // 2
    sub = lax.broadcasted_iota(jnp.int32, (8, 128), 0)
    lane = lax.broadcasted_iota(jnp.int32, (8, 128), 1)
    token_chip = lane >> 4
    owner_chip = ids >> 6
    chip_slot = ids & 63
    mine = (ids >> 5) == me
    fetch, quick_fetch, longest_f, crowded_f = slot_plan(owner_chip, token_chip, chip_slot, ids, chip, sub, lane)
    back, quick_back, longest_b, crowded_b = slot_plan(token_chip, owner_chip, lane & 15, None, chip, sub, lane)
    fits = jnp.logical_and(longest_f <= SLOTS_OUT, longest_b <= SLOTS_BACK)
    fits = jnp.logical_and(fits, crowded_f + crowded_b == 0)
    columns = {}
    for at, plan in ((0, fetch), (2, back), (5, quick_fetch), (7, quick_back)):
        for d, (leaves, out_slot, source, _, _) in enumerate(plan):
            columns[at + d] = by_row(leaves, out_slot, source, 32)
    for at, plan, slots in ((4, fetch, SLOTS_OUT), (9, quick_fetch, EXPRESS)):
        where = jnp.where(owner_chip == token_chip, chip_slot + 1, 0)
        for d in range(2):
            where = jnp.where(plan[d][3], 65 + d * slots + plan[d][4], where)
        columns[at] = by_row((lane >> 3) == me, lane & 7, where, 32)
    stays = jnp.logical_and(owner_chip == token_chip, token_chip == chip)
    line = lax.broadcasted_iota(jnp.int32, (128, 128), 1)
    lists = []
    for plan, slots in ((back, SLOTS_BACK), (quick_back, EXPRESS)):
        landing = jnp.where(stays, 2 * slots + (lane & 15), -1)
        for d in range(2):
            landing = jnp.where(plan[d][3], d * slots + plan[d][4], landing)
        if not lists:
            wanted = jnp.logical_and(landing >= 0, mine)
            count = bcast(jnp.sum(jnp.where(wanted, 1, 0), axis=1, keepdims=True))
            ahead = jnp.transpose(tall(jnp.where(wanted, lane, 128)))
            rank = bcast(jnp.sum(jnp.where(ahead < line, 1, 0), axis=0, keepdims=True))
        entry = jnp.where(wanted, rank * 4096 + landing * 32 + (ids & 31), -1)
        entry = jnp.transpose(tall(entry))
        lists.append(bcast(jnp.sum(jnp.where((entry >> 12) == line, entry & 4095, 0), axis=0, keepdims=True)))
    wide_lane = lax.broadcasted_iota(jnp.int32, (32, 128), 1)
    table = jnp.concatenate([jnp.where(fits, 1, 0)] * 4, axis=0)
    for i, column in columns.items():
        table = jnp.where(wide_lane == i, jnp.broadcast_to(column, (32, 128)), table)
    last = jnp.where(sub == 0, lists[0], jnp.where(sub == 1, lists[1], count))
    return jnp.concatenate([table, last], axis=0)


def wait_bytes(ref, sem):
    pltpu.make_async_copy(ref, ref, sem).wait()


def ring_kernel(hw, dw, ids_ref, hid_hbm, og_hbm, a_hbm, b_hbm, flag_ref, table_ref, fac_hbm, back_ref, fin_a, fin_b,
                idbuf, table, fac_a, fac_b, proj_ref, hid, og, grads_a, grads_b,
                own_ra, own_rb, own_sa, own_sb, picked_a, picked_b, items_a, items_b,
                stage_fa, stage_fb, stage_ra, stage_rb, got_fa, got_fb, got_ra, got_rb, kept_fa, kept_fb, kept_ra, kept_rb,
                part, parts, sums, loc, ids_sem, sib, swap_sem, ring_send, ring_recv, fwd, psum_sem):
    me = lax.axis_index("dp")
    t = lax.axis_index("tensor")
    chip = me // 2
    core = me % 2
    other = 1 - core
    sibling = {"dp": chip * 2 + other}
    mine32 = pl.ds(pl.multiple_of(core * OWNED, OWNED), OWNED)
    mine8 = pl.ds(pl.multiple_of(core * NBLK, NBLK), NBLK)

    def far(src, dst, send, recv, where):
        return pltpu.make_async_remote_copy(
            src_ref=src, dst_ref=dst, send_sem=send, recv_sem=recv, device_id=where, device_id_type=MESH
        )

    def lanes(width, which):
        return pl.ds(pl.multiple_of(which * width, 128), width)

    def cut(ref, width, which):
        return ref.at[:, :, lanes(width, which)]

    barrier = pltpu.get_barrier_semaphore()
    for o in range(1, NDP):
        pl.semaphore_signal(barrier, inc=1, device_id={"dp": lax.rem(me + o, NDP)}, device_id_type=MESH)
    for o in range(1, NT):
        pl.semaphore_signal(barrier, inc=1, device_id={"tensor": lax.rem(t + o, NT)}, device_id_type=MESH)
    owns = ((b_hbm, own_rb, dw, core), (a_hbm, own_ra, hw, core), (b_hbm, own_sb, dw, other), (a_hbm, own_sa, hw, other))
    for i, (ref, dst, width, which) in enumerate(owns):
        pltpu.make_async_copy(cut(ref, width, which), dst.at[mine32], loc.at[i]).start()
    pltpu.make_async_copy(og_hbm, og, loc.at[4]).start()
    pltpu.make_async_copy(hid_hbm, hid, loc.at[5]).start()

    lane = lax.broadcasted_iota(jnp.int32, (8, 128), 1)
    mine_ids = jnp.zeros((8, 128), jnp.int32)
    for j in range(NBLK):
        mine_ids = jnp.where(lane == me * NBLK + j, ids_ref[j], mine_ids)
    idbuf[me] = mine_ids
    pl.semaphore_wait(barrier, NDP - 1 + NT - 1)

    for o in range(1, NDP):
        far(idbuf.at[me], idbuf.at[me], ids_sem.at[0], ids_sem.at[1], {"dp": lax.rem(me + o, NDP)}).start()
    for i, (ref, dst, width, which) in enumerate(owns):
        far(cut(ref, width, 1 - which), dst.at[mine32], sib.at[0, i], sib.at[1, i], sibling).start()

    def own_ready(i):
        dst = owns[i][1].at[pl.ds(0, OWNED)]
        wait_bytes(dst, loc.at[i])
        wait_bytes(dst, sib.at[1, i])

    wait_bytes(idbuf.at[pl.ds(0, NDP - 1)], ids_sem.at[1])
    ids = idbuf[0]
    for i in range(1, NDP):
        ids = ids + idbuf[i]
    table_ref[...] = make_tables(ids, me)
    to_smem = pltpu.make_async_copy(table_ref, table, loc.at[6])
    to_smem.start()
    to_smem.wait()

    def stream(index, column, own, stage, got, kept, land_at, keep_local, pieces, free):
        count = own.shape[0]
        slots = stage.shape[1]
        everything = kept.at[pl.ds(0, 2 * slots)]

        def copy(d, q):
            p, n, hops = pieces[q]
            return far(
                stage.at[d, pl.ds(p, n)],
                got.at[d, pl.ds(p, n)],
                ring_send.at[index],
                ring_recv.at[index, d, q],
                {"dp": lax.rem(chip + (hops if d == 0 else NCHIP - hops), NCHIP) * 2 + core},
            )

        def landed(d, q):
            copy(d, q).wait_recv()
            p, n, _ = pieces[q]
            there = land_at(pl.ds(d * slots + p, n))
            far(got.at[d, pl.ds(p, n)], there, fwd.at[index, 1], fwd.at[index, 2], sibling).start()
            if keep_local:
                pltpu.make_async_copy(got.at[d, pl.ds(p, n)], there, fwd.at[index, 0]).start()
            kept[pl.ds(d * slots + p, n)] = got[d, pl.ds(p, n)]

        def send(d, q):
            p, n, _ = pieces[q]
            for i in range(n):
                code = table[p + i, column + d]
                value = own[jnp.clip(code - 1, 0, count - 1)]
                if q >= free:
                    passed = kept[d * slots + jnp.clip(code - 65, 0, slots - 1)]
                    value = jnp.where(code > 64, passed, value)
                stage[d, p + i] = value
            copy(d, q).start()

        def arrived():
            if keep_local:
                wait_bytes(everything, fwd.at[index, 0])
            wait_bytes(everything, fwd.at[index, 2])

        def finish():
            wait_bytes(stage, ring_send.at[index])
            wait_bytes(everything, fwd.at[index, 1])

        return landed, send, arrived, finish

    def hop_stream(index, column, own, stage, got, kept, land_at, keep_local):
        slots = stage.shape[1]
        pieces = [(p, min(2, slots - p), 1) for p in range(0, slots, 2)]
        behind = LAG // 2
        landed, send, arrived, finish = stream(
            index, column, own, stage, got, kept, land_at, keep_local, pieces, behind
        )

        def step(m):
            for d in range(2):
                if m >= behind:
                    landed(d, m - behind)
                if m < len(pieces):
                    send(d, m)

        return step, arrived, finish

    def express_stream(index, column, own, stage, got, kept, land_at, keep_local):
        pieces = [(0, TWO_FIRST, 2), (TWO, ONE_FIRST, 1), (TWO_FIRST, TWO - TWO_FIRST, 2), (TWO + ONE_FIRST, ONE - ONE_FIRST, 1)]
        landed, send, arrived, finish = stream(
            index, column, own, stage, got, kept, land_at, keep_local, pieces, 2
        )

        def step(m):
            for d in range(2):
                for q in ((), (0,), (1, 2, 3))[m]:
                    landed(d, q)
                for q in ((0, 1), (2, 3), ())[m]:
                    send(d, q)

        return step, arrived, finish

    def play(order, steps, others):
        count = dict.fromkeys(steps, 0)
        for kind in order:
            if kind in others:
                others[kind]()
            else:
                steps[kind](count[kind])
                count[kind] += 1

    fa, fa_arrived, fa_finish = hop_stream(
        0, 0, own_ra, stage_fa, got_fa, kept_fa, lambda s: picked_a.at[s], False
    )
    fb, fb_arrived, fb_finish = express_stream(
        1, 5, own_rb, stage_fb, got_fb, kept_fb, lambda s: picked_b.at[s], False
    )
    ra, ra_arrived, ra_finish = hop_stream(
        2, 2, items_a, stage_ra, got_ra, kept_ra, lambda s: fin_a.at[s, :, lanes(hw, core)], True
    )
    rb, rb_arrived, rb_finish = express_stream(
        3, 7, items_b, stage_rb, got_rb, kept_rb, lambda s: fin_b.at[s, :, lanes(dw, core)], True
    )

    def choose(j, column, fac, own_r, own_s, kept, picked, width):
        code = table[j, column]
        near = code <= 64
        at = jnp.clip(code - 1, 0, 2 * OWNED - 1)
        away = jnp.clip(code - 65, 0, picked.shape[0] - 1)
        fac[j, :, lanes(width, core)] = jnp.where(near, own_r[at], kept[away])
        fac[j, :, lanes(width, other)] = jnp.where(near, own_s[at], picked[away])

    def project(i, fac, rows_ref):
        for j in range(NBLK):
            term = lax.dot_general(
                fac[j], rows_ref[pl.ds(j * BLOCK, BLOCK)], (((1,), (1,)), ((), ())),
                preferred_element_type=jnp.float32,
            )
            part[i, 2 * j] = term[:8]
            part[i, 2 * j + 1] = term[8:]

    def peers():
        return [lax.rem(t + o, NT) for o in range(1, NT)]

    def scatter(i):
        parts[i, t] = part[i, t]
        for peer in peers():
            far(part.at[i, peer], parts.at[i, t], psum_sem.at[i, 0], psum_sem.at[i, 1], {"tensor": peer}).start()

    def reduce(i):
        wait_bytes(parts.at[i, pl.ds(0, NT - 1)], psum_sem.at[i, 1])
        total = parts[i, 0]
        for n in range(1, NT):
            total = total + parts[i, n]
        sums[i, t] = total
        for peer in peers():
            far(sums.at[i, t], sums.at[i, t], psum_sem.at[i, 2], psum_sem.at[i, 3], {"tensor": peer}).start()

    def gather(i, out):
        wait_bytes(sums.at[i, pl.ds(0, NT - 1)], psum_sem.at[i, 3])
        for j in range(NBLK):
            out[j] = jnp.concatenate([sums[i, 2 * j], sums[i, 2 * j + 1]], axis=0).astype(jnp.bfloat16)

    def gradient(low, rows_ref, grads, width, which):
        for j in range(NBLK):
            grad = adapter_scale * jnp.dot(
                low[j], rows_ref[pl.ds(j * BLOCK, BLOCK), lanes(width, which)], preferred_element_type=jnp.float32
            )
            grads[j, :, lanes(width, which)] = grad.astype(jnp.bfloat16)

    def hand_over(i, low, rows_ref, grads, items, fin, width, slots):
        tail8 = pl.ds(2 * slots + core * NBLK, NBLK)
        gradient(low, rows_ref, grads, width, other)
        swap = far(cut(grads, width, other), items.at[mine8], swap_sem.at[i, 0], swap_sem.at[i, 1], sibling)
        swap.start()
        gradient(low, rows_ref, grads, width, core)
        items[mine8] = grads[:, :, lanes(width, core)]
        share = far(grads, fin.at[tail8], swap_sem.at[i, 2], swap_sem.at[i, 3], sibling)
        share.start()
        keep = pltpu.make_async_copy(grads, fin.at[tail8], swap_sem.at[i, 4])
        keep.start()
        return swap, share, keep

    def back_part():
        own_ready(2)
        fb_arrived()
        wait_bytes(og, loc.at[4])
        for j in range(NBLK):
            choose(j, 9, fac_b, own_rb, own_sb, kept_fb, picked_b, dw)
        project(0, fac_b, og)
        scatter(0)

    def proj_part():
        own_ready(3)
        fa_arrived()
        for j in range(NBLK):
            choose(j, 4, fac_a, own_ra, own_sa, kept_fa, picked_a, hw)
        project(1, fac_a, hid)
        scatter(1)
        pltpu.make_async_copy(fac_a, fac_hbm, loc.at[7]).start()

    moves_a, moves_b = [], []

    def give_a():
        wait_bytes(hid, loc.at[5])
        gather(0, back_ref)
        moves_a.extend(hand_over(0, back_ref, hid, grads_a, items_a, fin_a, hw, SLOTS_BACK))

    def give_b():
        gather(1, proj_ref)
        moves_b.extend(hand_over(1, proj_ref, og, grads_b, items_b, fin_b, dw, EXPRESS))

    own_ready(0)
    own_ready(1)
    play(
        ORDER,
        {"a": fa, "b": fb, "A": ra, "B": rb},
        {
            "P": back_part,
            "R": lambda: reduce(0),
            "H": give_a,
            "W": lambda: moves_a[0].wait_recv(),
            "Q": proj_part,
            "S": lambda: reduce(1),
            "G": give_b,
            "X": lambda: moves_b[0].wait_recv(),
        },
    )

    flag_ref[0] = table[0, FLAG]
    ra_arrived()
    rb_arrived()
    wait_bytes(fac_a, loc.at[7])
    for swap, share, keep in (moves_a, moves_b):
        swap.wait_send()
        share.wait()
        keep.wait()
    wait_bytes(idbuf.at[pl.ds(0, NDP - 1)], ids_sem.at[0])
    for i in range(4):
        wait_bytes(owns[i][1].at[pl.ds(0, OWNED)], sib.at[0, i])
    for i in range(2):
        wait_bytes(parts.at[i, pl.ds(0, NT - 1)], psum_sem.at[i, 0])
        wait_bytes(sums.at[i, pl.ds(0, NT - 1)], psum_sem.at[i, 2])
    fa_finish()
    fb_finish()
    ra_finish()
    rb_finish()


def last_kernel(table, fin_a, fin_b, fac, back, gh, ga, gb, acc_a, acc_b, buf_a, buf_b, ghb, gab, gbb, sems):
    count = table[34, 0]

    def arriving(p):
        return (
            pltpu.make_async_copy(fin_a.at[table[32, p] >> 5], buf_a.at[p], sems.at[0]),
            pltpu.make_async_copy(fin_b.at[table[33, p] >> 5], buf_b.at[p], sems.at[4]),
        )

    def loop(step):
        def run(p, carry):
            step(p)
            return carry

        lax.fori_loop(0, count, run, 0)

    def start(p):
        for copy in arriving(p):
            copy.start()

    def wait(p):
        for copy in arriving(p):
            copy.wait()

    loop(start)
    for j in range(NBLK):
        rows = pl.ds(j * BLOCK, BLOCK)
        rows_out = adapter_scale * lax.dot_general(
            back[j], fac[j], (((0,), (0,)), ((), ())), preferred_element_type=jnp.float32
        )
        ghb[rows] = rows_out.astype(jnp.bfloat16)
        pltpu.make_async_copy(ghb.at[rows], gh.at[rows], sems.at[1]).start()
    gab[...] = jnp.zeros_like(gab)
    gbb[...] = jnp.zeros_like(gbb)
    trio = ((acc_a, buf_a, gab), (acc_b, buf_b, gbb))

    def clear(p):
        for acc, _, _ in trio:
            acc[table[32, p] & 31] = jnp.zeros(acc.shape[1:], jnp.float32)

    def add(p):
        for acc, buf, _ in trio:
            acc[table[32, p] & 31] += buf[p].astype(jnp.float32)

    def store(p):
        for acc, _, out in trio:
            out[table[32, p] & 31] = acc[table[32, p] & 31].astype(jnp.bfloat16)

    loop(clear)
    loop(wait)
    loop(add)
    loop(store)
    ca = pltpu.make_async_copy(gab, ga, sems.at[2])
    cb = pltpu.make_async_copy(gbb, gb, sems.at[3])
    ca.start()
    cb.start()
    pltpu.make_async_copy(ghb, gh, sems.at[1]).wait()
    ca.wait()
    cb.wait()


def shards(hidden, output_gradient, block_adapter_index, adapter_down_factors, adapter_up_factors):
    rows, ff_local = hidden.shape
    d_local = output_gradient.shape[1]
    hw, dw = ff_local // 2, d_local // 2
    bf16, f32 = jnp.bfloat16, jnp.float32
    vmem = pl.BlockSpec(memory_space=pltpu.VMEM)
    smem = pl.BlockSpec(memory_space=pltpu.SMEM)
    anywhere = pl.BlockSpec(memory_space=pl.ANY)
    dma = pltpu.SemaphoreType.DMA
    rank = ADAPTER_RANK
    streams = [
        pltpu.VMEM((2, slots, rank, width), bf16)
        for slots, width in ((SLOTS_OUT, hw), (EXPRESS, dw), (SLOTS_BACK, hw), (EXPRESS, dw))
    ]
    scratch = [
        pltpu.VMEM((NDP, 8, 128), jnp.int32),
        pltpu.SMEM((40, 128), jnp.int32),
        pltpu.VMEM((NBLK, rank, ff_local), bf16),
        pltpu.VMEM((NBLK, rank, d_local), bf16),
        pltpu.VMEM((NBLK, rank, BLOCK), bf16),
        pltpu.VMEM((rows, ff_local), bf16),
        pltpu.VMEM((rows, d_local), bf16),
        pltpu.VMEM((NBLK, rank, ff_local), bf16),
        pltpu.VMEM((NBLK, rank, d_local), bf16),
        pltpu.VMEM((2 * OWNED, rank, hw), bf16),
        pltpu.VMEM((2 * OWNED, rank, dw), bf16),
        pltpu.VMEM((2 * OWNED, rank, hw), bf16),
        pltpu.VMEM((2 * OWNED, rank, dw), bf16),
        pltpu.VMEM((2 * SLOTS_OUT, rank, hw), bf16),
        pltpu.VMEM((2 * EXPRESS, rank, dw), bf16),
        pltpu.VMEM((2 * NBLK, rank, hw), bf16),
        pltpu.VMEM((2 * NBLK, rank, dw), bf16),
        *streams,
        *streams,
        pltpu.VMEM((2 * SLOTS_OUT, rank, hw), bf16),
        pltpu.VMEM((2 * EXPRESS, rank, dw), bf16),
        pltpu.VMEM((2 * SLOTS_BACK, rank, hw), bf16),
        pltpu.VMEM((2 * EXPRESS, rank, dw), bf16),
        pltpu.VMEM((2, NT, 8, BLOCK), f32),
        pltpu.VMEM((2, NT, 8, BLOCK), f32),
        pltpu.VMEM((2, NT, 8, BLOCK), f32),
        dma((8,)),
        dma((2,)),
        dma((2, 4)),
        dma((2, 5)),
        dma((4,)),
        dma((4, 2, max(SLOTS_OUT, SLOTS_BACK))),
        dma((4, 3)),
        dma((2, 4)),
    ]
    flag, table, fac, back, fin_a, fin_b = pl.pallas_call(
        functools.partial(ring_kernel, hw, dw),
        name="ring",
        out_shape=(
            jax.ShapeDtypeStruct((1,), jnp.int32),
            jax.ShapeDtypeStruct((40, 128), jnp.int32),
            jax.ShapeDtypeStruct((NBLK, rank, ff_local), bf16),
            jax.ShapeDtypeStruct((NBLK, rank, BLOCK), bf16),
            jax.ShapeDtypeStruct((NFIN, rank, ff_local), bf16),
            jax.ShapeDtypeStruct((NFIN, rank, d_local), bf16),
        ),
        in_specs=[smem] + [anywhere] * 4,
        out_specs=(smem, vmem, anywhere, vmem, anywhere, anywhere),
        scratch_shapes=scratch,
        compiler_params=pltpu.CompilerParams(
            collective_id=0, has_side_effects=True, vmem_limit_bytes=VMEM_LIMIT
        ),
    )(block_adapter_index, hidden, output_gradient, adapter_down_factors, adapter_up_factors)

    def finish(*_):
        return pl.pallas_call(
            last_kernel,
            name="finish",
            out_shape=(
                jax.ShapeDtypeStruct((rows, ff_local), bf16),
                jax.ShapeDtypeStruct(adapter_down_factors.shape, bf16),
                jax.ShapeDtypeStruct(adapter_up_factors.shape, bf16),
            ),
            in_specs=[smem, anywhere, anywhere, vmem, vmem],
            out_specs=(anywhere, anywhere, anywhere),
            scratch_shapes=[
                pltpu.VMEM((OWNED, rank, ff_local), f32),
                pltpu.VMEM((OWNED, rank, d_local), f32),
                pltpu.VMEM((NFIN, rank, ff_local), bf16),
                pltpu.VMEM((NFIN, rank, d_local), bf16),
                pltpu.VMEM((rows, ff_local), bf16),
                pltpu.VMEM((OWNED, rank, ff_local), bf16),
                pltpu.VMEM((OWNED, rank, d_local), bf16),
                dma((5,)),
            ],
            compiler_params=pltpu.CompilerParams(vmem_limit_bytes=VMEM_LIMIT),
        )(table, fin_a, fin_b, fac, back)

    return lax.cond(
        flag[0] > 0,
        finish,
        general,
        hidden,
        output_gradient,
        block_adapter_index,
        adapter_down_factors,
        adapter_up_factors,
    )


def solution(mesh):
    placed = (
        P("dp", "tensor"),
        P("dp", "tensor"),
        P("dp"),
        P("dp", None, "tensor"),
        P("dp", None, "tensor"),
    )
    return jax.shard_map(
        shards,
        mesh=mesh,
        in_specs=placed,
        out_specs=(P("dp", "tensor"), P("dp", None, "tensor"), P("dp", None, "tensor")),
        check_vma=False,
    )
```

```python
import functools

import jax
import jax.numpy as jnp
from jax import lax
from jax.experimental import pallas as pl
from jax.experimental.pallas import tpu as pltpu
from jax.sharding import PartitionSpec as P

ADAPTER_RANK = 16
BLOCK = 128
CAP = 2
MESH = pl.DeviceIdType.MESH
NDP = 16
NCHIP = 8
NT = 16
NBLK = 8
OWNED = 32
SLOTS_OUT = 25
SLOTS_BACK = 26
LAG = 6
TWO_FIRST, TWO = 8, 13
ONE_FIRST, ONE = 3, 10
EXPRESS = TWO + ONE
NFIN = 2 * max(SLOTS_BACK, EXPRESS) + 16
FLAG = 12
ORDER = "baabaaabaPaaaaRaaaHaaaWAAQAAAASAAAAGAXBAAABAAB"
VMEM_LIMIT = 56 * 1024 * 1024


adapter_scale = 2.0


def general(hidden, output_gradient, block_adapter_index, adapter_down_factors, adapter_up_factors):
    dp_size = lax.axis_size("dp")
    my_index = lax.axis_index("dp")
    block_count = block_adapter_index.shape[0]
    owned_adapter_count = adapter_down_factors.shape[0]
    ff_local = hidden.shape[1]
    d_local = output_gradient.shape[1]
    slot_count = dp_size * CAP
    all_ids = lax.all_gather(block_adapter_index, "dp", axis=0, tiled=True).reshape(
        dp_size, block_count
    )
    owners = all_ids // owned_adapter_count
    local_ids = all_ids % owned_adapter_count
    same_owner = owners[:, :, None] == owners[:, None, :]
    block_range = jnp.arange(block_count, dtype=jnp.int32)
    earlier = block_range[None, :] < block_range[:, None]
    rank_in = jnp.sum(jnp.logical_and(same_owner, earlier[None, :, :]), axis=2)
    cap_range = jnp.arange(CAP, dtype=jnp.int32)
    chosen = jnp.logical_and(
        (owners == my_index)[:, None, :], rank_in[:, None, :] == cap_range[None, :, None]
    )
    owned_range = jnp.arange(owned_adapter_count, dtype=jnp.int32)
    local_match = local_ids[:, :, None] == owned_range[None, None, :]
    selection_table = jnp.sum(
        jnp.logical_and(chosen[:, :, :, None], local_match[:, None, :, :]), axis=2
    )
    selection_table = selection_table.reshape(slot_count, owned_adapter_count).astype(jnp.bfloat16)
    send_a = jnp.einsum(
        "dz,zeg->deg", selection_table, adapter_down_factors, preferred_element_type=jnp.float32
    ).astype(jnp.bfloat16)
    send_b = jnp.einsum(
        "ge,elq->glq", selection_table, adapter_up_factors, preferred_element_type=jnp.float32
    ).astype(jnp.bfloat16)
    send_a = send_a.reshape(dp_size, CAP, ADAPTER_RANK, ff_local)
    send_b = send_b.reshape(dp_size, CAP, ADAPTER_RANK, d_local)
    fetched_a, fetched_b = (
        lax.all_to_all(send_a, "dp", split_axis=0, concat_axis=0, tiled=True),
        lax.all_to_all(send_b, "dp", split_axis=0, concat_axis=0, tiled=True),
    )
    fetched_a = fetched_a.reshape(slot_count, ADAPTER_RANK, ff_local)
    fetched_b = fetched_b.reshape(slot_count, ADAPTER_RANK, d_local)
    my_owners = jnp.take(owners, my_index, axis=0)
    my_ranks = jnp.take(rank_in, my_index, axis=0)
    my_slots = my_owners * CAP + my_ranks
    down_factor = jnp.take(fetched_a, my_slots, axis=0)
    up_factor = jnp.take(fetched_b, my_slots, axis=0)
    hid_blocks = hidden.reshape(block_count, BLOCK, ff_local)
    out_blocks = output_gradient.reshape(block_count, BLOCK, d_local)
    proj_part = jnp.einsum(
        "jtf,jrf->jtr", hid_blocks, down_factor, preferred_element_type=jnp.float32
    )
    back_part = jnp.einsum(
        "jtd,jrd->jtr", out_blocks, up_factor, preferred_element_type=jnp.float32
    )
    proj, back = lax.psum((proj_part, back_part), "tensor")
    projected_up = proj.astype(jnp.bfloat16)
    backward_up = back.astype(jnp.bfloat16)
    block_down_gradient = (
        adapter_scale
        * jnp.einsum("jtr,jtf->jrf", backward_up, hid_blocks, preferred_element_type=jnp.float32)
    ).astype(jnp.bfloat16)
    block_up_gradient = (
        adapter_scale
        * jnp.einsum("jtr,jtd->jrd", projected_up, out_blocks, preferred_element_type=jnp.float32)
    ).astype(jnp.bfloat16)
    gradient_rows = adapter_scale * jnp.einsum(
        "jtr,jrf->jtf", backward_up, down_factor, preferred_element_type=jnp.float32
    )
    grad_hidden = gradient_rows.astype(jnp.bfloat16).reshape(block_count * BLOCK, ff_local)
    slot_range = jnp.arange(slot_count, dtype=jnp.int32)
    place_table = (slot_range[:, None] == my_slots[None, :]).astype(jnp.bfloat16)
    back_a = jnp.einsum(
        "kj,jrf->krf", place_table, block_down_gradient, preferred_element_type=jnp.float32
    ).astype(jnp.bfloat16)
    back_bb = jnp.einsum(
        "kj,jrd->krd", place_table, block_up_gradient, preferred_element_type=jnp.float32
    ).astype(jnp.bfloat16)
    back_a = back_a.reshape(dp_size, CAP, ADAPTER_RANK, ff_local)
    back_bb = back_bb.reshape(dp_size, CAP, ADAPTER_RANK, d_local)
    recv_a, recv_b = (
        lax.all_to_all(back_a, "dp", split_axis=0, concat_axis=0, tiled=True),
        lax.all_to_all(back_bb, "dp", split_axis=0, concat_axis=0, tiled=True),
    )
    sum_table = jnp.transpose(selection_table)
    grad_a = jnp.einsum(
        "ak,krf->arf",
        sum_table,
        recv_a.reshape(slot_count, ADAPTER_RANK, ff_local),
        preferred_element_type=jnp.float32,
    )
    grad_b = jnp.einsum(
        "ak,krd->ard",
        sum_table,
        recv_b.reshape(slot_count, ADAPTER_RANK, d_local),
        preferred_element_type=jnp.float32,
    )
    return (grad_hidden, grad_a.astype(jnp.bfloat16), grad_b.astype(jnp.bfloat16))


def bcast(x, shape=(8, 128)):
    return jnp.broadcast_to(x, shape)


def pick_row(x, sub, row):
    return bcast(jnp.sum(jnp.where(sub == row, x, 0), axis=0, keepdims=True))


def turn(x, by):
    by = by % 8
    return pltpu.roll(x, by, 0) if by else x


def tall(x):
    return jnp.concatenate([x] * 16, axis=0)


def slot_plan(src, dst, own_index, shared, chip, sub, lane):
    ahead = (dst - src) & 7
    low = lax.broadcasted_iota(jnp.int32, (128, 128), 0)
    line = lax.broadcasted_iota(jnp.int32, (128, 128), 1)

    def per_chip(mask):
        return bcast(jnp.sum(jnp.where(jnp.logical_and(src == sub, mask), 1, 0), axis=1, keepdims=True))

    def over_all(x):
        return bcast(jnp.sum(x, axis=0, keepdims=True))

    one, two, three, across, five, six, seven = [per_chip(ahead == d) for d in range(1, 8)]
    load_p = one + two + three + turn(two + three, 1) + turn(three, 2)
    load_m = seven + six + five + turn(six + five, -1) + turn(five, -2)
    forward = jnp.zeros((8, 128), jnp.int32)
    for phase in range(4):
        worst_p = jnp.maximum(load_p, turn(load_p, -1))
        worst_p = jnp.maximum(worst_p, turn(worst_p, -2))
        worst_m = jnp.maximum(load_m, turn(load_m, 1))
        worst_m = jnp.maximum(worst_m, turn(worst_m, 2))
        share = jnp.minimum(jnp.maximum((across + worst_m - worst_p + 1) >> 1, 0), across)
        chosen = (sub & 3) == phase
        share_p = jnp.where(chosen, share, 0)
        share_m = jnp.where(chosen, across - share, 0)
        forward = forward + share_p
        share_p = share_p + turn(share_p, 1)
        load_p = load_p + share_p + turn(share_p, 2)
        share_m = share_m + turn(share_m, -1)
        load_m = load_m + share_m + turn(share_m, -2)
    opposite = tall(jnp.where(ahead == 4, src, 8))
    nth = over_all(jnp.where(jnp.logical_and(jnp.transpose(opposite) == opposite, low < line), 1, 0))
    quota = over_all(jnp.where(src == sub, forward, 0))
    plus = jnp.logical_and(ahead > 0, jnp.logical_or(ahead < 4, jnp.logical_and(ahead == 4, nth < quota)))
    minus = jnp.logical_or(ahead > 4, jnp.logical_and(ahead == 4, nth >= quota))
    dist = jnp.where(plus, ahead, jnp.where(minus, 8 - ahead, 0))
    group = jnp.where(ahead > 0, src * 2 + jnp.where(minus, 1, 0), 16)
    order = group * 1024 + (4 - dist) * 128 + lane
    wide = tall(order)

    def ranked(active):
        column = jnp.transpose(tall(jnp.where(active, order, 32767)))
        return over_all(jnp.where(jnp.logical_and((column >> 10) == (wide >> 10), column < wide), 1, 0))

    everyone = lane >= 0
    plain_rank = ranked(everyone)
    if shared is None:
        active, rank = everyone, plain_rank
    else:
        packed = tall(shared * 32768 + order)
        column = jnp.transpose(packed)
        same = (packed >> 10) == (column >> 10)
        active = over_all(jnp.where(jnp.logical_and(same, column < packed), 1, 0)) == 0
        led = jnp.transpose(tall(jnp.where(active, ranked(active), 0)))
        rank = over_all(jnp.where(same, led, 0))
    hops = []
    express = []
    longest = jnp.zeros((8, 128), jnp.int32)
    crowded = jnp.zeros((8, 128), jnp.int32)
    for sign, act in ((1, plus), (-1, minus)):
        age = (sign * (chip - src)) & 7
        arrives = jnp.logical_and(act, age == dist)
        goes = jnp.logical_and(act, active)
        counts = [per_chip(jnp.logical_and(goes, dist > h)) for h in range(4)]
        starts = [jnp.zeros((8, 128), jnp.int32)]
        for h in range(1, 4):
            starts.append(
                jnp.maximum(
                    starts[h - 1] + turn(counts[h - 1], sign * (h - 1)),
                    turn(starts[h - 1], sign) + LAG,
                )
            )
        for h in range(4):
            here = turn(counts[h], sign * h)
            longest = jnp.maximum(longest, jnp.where(here > 0, starts[h] + here, 0))
        out_start = jnp.zeros((8, 128), jnp.int32)
        in_start = jnp.zeros((8, 128), jnp.int32)
        before_chip = (chip - sign) & 7
        for h in range(4):
            out_start = jnp.where(age == h, pick_row(starts[h], sub, chip), out_start)
            in_start = jnp.where(age == h + 1, pick_row(starts[h], sub, before_chip), in_start)
        leaves = jnp.logical_and(goes, age < dist)
        in_slot = in_start + rank
        source = jnp.where(age == 0, own_index + 1, 65 + in_slot)
        hops.append((leaves, out_start + rank, source, arrives, in_slot))

        if shared is not None:
            counts = [per_chip(jnp.logical_and(act, dist > h)) for h in range(4)]
        single, third = counts[0] - counts[1], counts[2] - counts[3]
        two_start = jnp.maximum(counts[1], TWO_FIRST)
        one_start = jnp.maximum(single, ONE_FIRST)
        passing4 = turn(counts[3], 2 * sign)
        passing3 = turn(third, 2 * sign)
        two_end = jnp.where(passing4 > 0, two_start + passing4, counts[1])
        one_end = jnp.where(passing3 > 0, one_start + passing3, single)
        full = jnp.logical_or(
            jnp.logical_or(two_end > TWO, one_end > ONE), counts[2] > TWO_FIRST
        )
        crowded = jnp.maximum(crowded, jnp.where(full, 1, 0))
        far_before = over_all(jnp.where(src == sub, counts[1], 0))
        four_before = over_all(jnp.where(src == sub, counts[3], 0))
        own = age == 0
        passes = age == 2
        as_two = jnp.logical_and(own, dist >= 2)
        as_one = jnp.logical_and(own, dist == 1)
        on_two = jnp.logical_and(passes, dist == 4)
        on_one = jnp.logical_and(passes, dist == 3)
        leaves = jnp.logical_and(
            act, jnp.logical_or(jnp.logical_or(as_two, as_one), jnp.logical_or(on_two, on_one))
        )
        near_slot = TWO + plain_rank - far_before
        third_slot = TWO + plain_rank - four_before
        out_slot = jnp.where(as_one, near_slot, plain_rank)
        out_slot = jnp.where(on_two, pick_row(two_start, sub, chip) + plain_rank, out_slot)
        out_slot = jnp.where(on_one, pick_row(one_start, sub, chip) + third_slot, out_slot)
        source = jnp.where(own, own_index + 1, 65 + plain_rank)
        in_slot = jnp.where(dist == 1, near_slot, plain_rank)
        in_slot = jnp.where(dist == 3, pick_row(one_start, sub, before_chip) + third_slot, in_slot)
        in_slot = jnp.where(
            dist == 4, pick_row(two_start, sub, (chip - 2 * sign) & 7) + plain_rank, in_slot
        )
        express.append((leaves, out_slot, source, arrives, in_slot))
    return hops, express, bcast(jnp.max(longest, axis=0, keepdims=True)), over_all(crowded)


def by_row(mask, place, value, rows):
    reps = rows // 8
    wide = [jnp.concatenate([v] * reps, axis=0) for v in (jnp.where(mask, place, -1), value)]
    sub = lax.broadcasted_iota(jnp.int32, (rows, 128), 0)
    return jnp.sum(jnp.where(wide[0] == sub, wide[1], 0), axis=1, keepdims=True)


def make_tables(ids, me):
    chip = me // 2
    sub = lax.broadcasted_iota(jnp.int32, (8, 128), 0)
    lane = lax.broadcasted_iota(jnp.int32, (8, 128), 1)
    token_chip = lane >> 4
    owner_chip = ids >> 6
    chip_slot = ids & 63
    mine = (ids >> 5) == me
    fetch, quick_fetch, longest_f, crowded_f = slot_plan(owner_chip, token_chip, chip_slot, ids, chip, sub, lane)
    back, quick_back, longest_b, crowded_b = slot_plan(token_chip, owner_chip, lane & 15, None, chip, sub, lane)
    fits = jnp.logical_and(longest_f <= SLOTS_OUT, longest_b <= SLOTS_BACK)
    fits = jnp.logical_and(fits, crowded_f + crowded_b == 0)
    columns = {}
    for at, plan in ((0, fetch), (2, back), (5, quick_fetch), (7, quick_back)):
        for d, (leaves, out_slot, source, _, _) in enumerate(plan):
            columns[at + d] = by_row(leaves, out_slot, source, 32)
    for at, plan, slots in ((4, fetch, SLOTS_OUT), (9, quick_fetch, EXPRESS)):
        where = jnp.where(owner_chip == token_chip, chip_slot + 1, 0)
        for d in range(2):
            where = jnp.where(plan[d][3], 65 + d * slots + plan[d][4], where)
        columns[at] = by_row((lane >> 3) == me, lane & 7, where, 32)
    stays = jnp.logical_and(owner_chip == token_chip, token_chip == chip)
    line = lax.broadcasted_iota(jnp.int32, (128, 128), 1)
    lists = []
    for plan, slots in ((back, SLOTS_BACK), (quick_back, EXPRESS)):
        landing = jnp.where(stays, 2 * slots + (lane & 15), -1)
        for d in range(2):
            landing = jnp.where(plan[d][3], d * slots + plan[d][4], landing)
        if not lists:
            wanted = jnp.logical_and(landing >= 0, mine)
            count = bcast(jnp.sum(jnp.where(wanted, 1, 0), axis=1, keepdims=True))
            ahead = jnp.transpose(tall(jnp.where(wanted, lane, 128)))
            rank = bcast(jnp.sum(jnp.where(ahead < line, 1, 0), axis=0, keepdims=True))
        entry = jnp.where(wanted, rank * 4096 + landing * 32 + (ids & 31), -1)
        entry = jnp.transpose(tall(entry))
        lists.append(bcast(jnp.sum(jnp.where((entry >> 12) == line, entry & 4095, 0), axis=0, keepdims=True)))
    wide_lane = lax.broadcasted_iota(jnp.int32, (32, 128), 1)
    table = jnp.concatenate([jnp.where(fits, 1, 0)] * 4, axis=0)
    for i, column in columns.items():
        table = jnp.where(wide_lane == i, jnp.broadcast_to(column, (32, 128)), table)
    last = jnp.where(sub == 0, lists[0], jnp.where(sub == 1, lists[1], count))
    return jnp.concatenate([table, last], axis=0)


def wait_bytes(ref, sem):
    pltpu.make_async_copy(ref, ref, sem).wait()


def ring_kernel(hw, dw, ids_ref, hid_hbm, og_hbm, a_hbm, b_hbm, flag_ref, list_ref, fac_hbm, back_ref, fin_a, fin_b,
                idbuf, table_ref, table, fac_a, fac_b, proj_ref, hid, og, grads_a, grads_b,
                own_ra, own_rb, own_sa, own_sb, picked_a, picked_b, items_a, items_b,
                stage_fa, stage_fb, stage_ra, stage_rb, got_fa, got_fb, got_ra, got_rb, kept_fa, kept_fb, kept_ra, kept_rb,
                part, parts, sums, loc, ids_sem, sib, swap_sem, ring_send, ring_recv, fwd, psum_sem):
    me = lax.axis_index("dp")
    t = lax.axis_index("tensor")
    chip = me // 2
    core = me % 2
    other = 1 - core
    sibling = {"dp": chip * 2 + other}
    mine32 = pl.ds(pl.multiple_of(core * OWNED, OWNED), OWNED)
    mine8 = pl.ds(pl.multiple_of(core * NBLK, NBLK), NBLK)

    def far(src, dst, send, recv, where):
        return pltpu.make_async_remote_copy(
            src_ref=src, dst_ref=dst, send_sem=send, recv_sem=recv, device_id=where, device_id_type=MESH
        )

    def lanes(width, which):
        return pl.ds(pl.multiple_of(which * width, 128), width)

    def cut(ref, width, which):
        return ref.at[:, :, lanes(width, which)]

    barrier = pltpu.get_barrier_semaphore()
    for o in range(1, NDP):
        pl.semaphore_signal(barrier, inc=1, device_id={"dp": lax.rem(me + o, NDP)}, device_id_type=MESH)
    for o in range(1, NT):
        pl.semaphore_signal(barrier, inc=1, device_id={"tensor": lax.rem(t + o, NT)}, device_id_type=MESH)
    owns = ((b_hbm, own_rb, dw, core), (a_hbm, own_ra, hw, core), (b_hbm, own_sb, dw, other), (a_hbm, own_sa, hw, other))
    for i, (ref, dst, width, which) in enumerate(owns):
        pltpu.make_async_copy(cut(ref, width, which), dst.at[mine32], loc.at[i]).start()
    pltpu.make_async_copy(og_hbm, og, loc.at[4]).start()
    pltpu.make_async_copy(hid_hbm, hid, loc.at[5]).start()

    lane = lax.broadcasted_iota(jnp.int32, (8, 128), 1)
    mine_ids = jnp.zeros((8, 128), jnp.int32)
    for j in range(NBLK):
        mine_ids = jnp.where(lane == me * NBLK + j, ids_ref[j], mine_ids)
    idbuf[me] = mine_ids
    pl.semaphore_wait(barrier, NDP - 1 + NT - 1)

    for o in range(1, NDP):
        far(idbuf.at[me], idbuf.at[me], ids_sem.at[0], ids_sem.at[1], {"dp": lax.rem(me + o, NDP)}).start()
    for i, (ref, dst, width, which) in enumerate(owns):
        far(cut(ref, width, 1 - which), dst.at[mine32], sib.at[0, i], sib.at[1, i], sibling).start()

    def own_ready(i):
        dst = owns[i][1].at[pl.ds(0, OWNED)]
        wait_bytes(dst, loc.at[i])
        wait_bytes(dst, sib.at[1, i])

    wait_bytes(idbuf.at[pl.ds(0, NDP - 1)], ids_sem.at[1])
    ids = idbuf[0]
    for i in range(1, NDP):
        ids = ids + idbuf[i]
    tables = make_tables(ids, me)
    table_ref[...] = tables
    list_ref[...] = tables[32:]
    to_smem = pltpu.make_async_copy(table_ref, table, loc.at[6])
    to_smem.start()
    to_smem.wait()

    def stream(index, column, own, stage, got, kept, land_at, keep_local, pieces, free, paired):
        count = own.shape[0]
        slots = stage.shape[1]
        everything = kept.at[pl.ds(0, 2 * slots)]

        def copy(d, q):
            p, n, hops = pieces[q]
            return far(
                stage.at[d, pl.ds(p, n)],
                got.at[d, pl.ds(p, n)],
                ring_send.at[index],
                ring_recv.at[index, d, q],
                {"dp": lax.rem(chip + (hops if d == 0 else NCHIP - hops), NCHIP) * 2 + core},
            )

        def landed(d, q):
            copy(d, q).wait_recv()
            p, n, _ = pieces[q]
            kept[pl.ds(d * slots + p, n)] = got[d, pl.ds(p, n)]
            if paired and q % 2 == 0 and q + 1 < len(pieces):
                return
            if paired and q % 2:
                p, n = p - pieces[q - 1][1], n + pieces[q - 1][1]
            there = land_at(pl.ds(d * slots + p, n))
            far(got.at[d, pl.ds(p, n)], there, fwd.at[index, 1], fwd.at[index, 2], sibling).start()
            if keep_local:
                pltpu.make_async_copy(got.at[d, pl.ds(p, n)], there, fwd.at[index, 0]).start()

        def send(d, q):
            p, n, _ = pieces[q]
            for i in range(n):
                code = table[p + i, column + d]
                value = own[jnp.clip(code - 1, 0, count - 1)]
                if q >= free:
                    passed = kept[d * slots + jnp.clip(code - 65, 0, slots - 1)]
                    value = jnp.where(code > 64, passed, value)
                stage[d, p + i] = value
            copy(d, q).start()

        def arrived():
            if keep_local:
                wait_bytes(everything, fwd.at[index, 0])
            wait_bytes(everything, fwd.at[index, 2])

        def finish():
            wait_bytes(stage, ring_send.at[index])
            wait_bytes(everything, fwd.at[index, 1])

        return landed, send, arrived, finish

    def hop_stream(index, column, own, stage, got, kept, land_at, keep_local):
        slots = stage.shape[1]
        pieces = [(p, min(2, slots - p), 1) for p in range(0, slots, 2)]
        behind = LAG // 2
        landed, send, arrived, finish = stream(
            index, column, own, stage, got, kept, land_at, keep_local, pieces, behind, True
        )

        def step(m):
            for d in range(2):
                if m >= behind:
                    landed(d, m - behind)
                if m < len(pieces):
                    send(d, m)

        return step, arrived, finish

    def express_stream(index, column, own, stage, got, kept, land_at, keep_local):
        pieces = [(0, TWO_FIRST, 2), (TWO, ONE_FIRST, 1), (TWO_FIRST, TWO - TWO_FIRST, 2), (TWO + ONE_FIRST, ONE - ONE_FIRST, 1)]
        landed, send, arrived, finish = stream(
            index, column, own, stage, got, kept, land_at, keep_local, pieces, 2, False
        )

        def step(m):
            for d in range(2):
                for q in ((), (0,), (1, 2, 3))[m]:
                    landed(d, q)
                for q in ((0, 1), (2, 3), ())[m]:
                    send(d, q)

        return step, arrived, finish

    def play(order, steps, others):
        count = dict.fromkeys(steps, 0)
        for kind in order:
            if kind in others:
                others[kind]()
            else:
                steps[kind](count[kind])
                count[kind] += 1

    fa, fa_arrived, fa_finish = hop_stream(
        0, 0, own_ra, stage_fa, got_fa, kept_fa, lambda s: picked_a.at[s], False
    )
    fb, fb_arrived, fb_finish = express_stream(
        1, 5, own_rb, stage_fb, got_fb, kept_fb, lambda s: picked_b.at[s], False
    )
    ra, ra_arrived, ra_finish = hop_stream(
        2, 2, items_a, stage_ra, got_ra, kept_ra, lambda s: fin_a.at[s, :, lanes(hw, core)], True
    )
    rb, rb_arrived, rb_finish = express_stream(
        3, 7, items_b, stage_rb, got_rb, kept_rb, lambda s: fin_b.at[s, :, lanes(dw, core)], True
    )

    def choose(j, column, fac, own_r, own_s, kept, picked, width):
        code = table[j, column]
        near = code <= 64
        at = jnp.clip(code - 1, 0, 2 * OWNED - 1)
        away = jnp.clip(code - 65, 0, picked.shape[0] - 1)
        fac[j, :, lanes(width, core)] = jnp.where(near, own_r[at], kept[away])
        fac[j, :, lanes(width, other)] = jnp.where(near, own_s[at], picked[away])

    def project(i, fac, rows_ref):
        for j in range(NBLK):
            term = lax.dot_general(
                fac[j], rows_ref[pl.ds(j * BLOCK, BLOCK)], (((1,), (1,)), ((), ())),
                preferred_element_type=jnp.float32,
            )
            part[i, 2 * j] = term[:8]
            part[i, 2 * j + 1] = term[8:]

    def peers():
        return [lax.rem(t + o, NT) for o in range(1, NT)]

    def scatter(i):
        parts[i, t] = part[i, t]
        for peer in peers():
            far(part.at[i, peer], parts.at[i, t], psum_sem.at[i, 0], psum_sem.at[i, 1], {"tensor": peer}).start()

    def reduce(i):
        wait_bytes(parts.at[i, pl.ds(0, NT - 1)], psum_sem.at[i, 1])
        total = parts[i, 0]
        for n in range(1, NT):
            total = total + parts[i, n]
        sums[i, t] = total
        for peer in peers():
            far(sums.at[i, t], sums.at[i, t], psum_sem.at[i, 2], psum_sem.at[i, 3], {"tensor": peer}).start()

    def gather(i, out):
        wait_bytes(sums.at[i, pl.ds(0, NT - 1)], psum_sem.at[i, 3])
        for j in range(NBLK):
            out[j] = jnp.concatenate([sums[i, 2 * j], sums[i, 2 * j + 1]], axis=0).astype(jnp.bfloat16)

    def gradient(low, rows_ref, grads, width, which):
        for j in range(NBLK):
            grad = adapter_scale * jnp.dot(
                low[j], rows_ref[pl.ds(j * BLOCK, BLOCK), lanes(width, which)], preferred_element_type=jnp.float32
            )
            grads[j, :, lanes(width, which)] = grad.astype(jnp.bfloat16)

    def hand_over(i, low, rows_ref, grads, items, fin, width, slots):
        tail8 = pl.ds(2 * slots + core * NBLK, NBLK)
        gradient(low, rows_ref, grads, width, other)
        swap = far(cut(grads, width, other), items.at[mine8], swap_sem.at[i, 0], swap_sem.at[i, 1], sibling)
        swap.start()
        gradient(low, rows_ref, grads, width, core)
        items[mine8] = grads[:, :, lanes(width, core)]
        share = far(grads, fin.at[tail8], swap_sem.at[i, 2], swap_sem.at[i, 3], sibling)
        share.start()
        keep = pltpu.make_async_copy(grads, fin.at[tail8], swap_sem.at[i, 4])
        keep.start()
        return swap, share, keep

    def back_part():
        own_ready(2)
        fb_arrived()
        wait_bytes(og, loc.at[4])
        for j in range(NBLK):
            choose(j, 9, fac_b, own_rb, own_sb, kept_fb, picked_b, dw)
        project(0, fac_b, og)
        scatter(0)

    def proj_part():
        own_ready(3)
        fa_arrived()
        for j in range(NBLK):
            choose(j, 4, fac_a, own_ra, own_sa, kept_fa, picked_a, hw)
        project(1, fac_a, hid)
        scatter(1)
        pltpu.make_async_copy(fac_a, fac_hbm, loc.at[7]).start()

    moves_a, moves_b = [], []

    def give_a():
        wait_bytes(hid, loc.at[5])
        gather(0, back_ref)
        moves_a.extend(hand_over(0, back_ref, hid, grads_a, items_a, fin_a, hw, SLOTS_BACK))

    def give_b():
        gather(1, proj_ref)
        moves_b.extend(hand_over(1, proj_ref, og, grads_b, items_b, fin_b, dw, EXPRESS))

    own_ready(0)
    own_ready(1)
    play(
        ORDER,
        {"a": fa, "b": fb, "A": ra, "B": rb},
        {
            "P": back_part,
            "R": lambda: reduce(0),
            "H": give_a,
            "W": lambda: moves_a[0].wait_recv(),
            "Q": proj_part,
            "S": lambda: reduce(1),
            "G": give_b,
            "X": lambda: moves_b[0].wait_recv(),
        },
    )

    flag_ref[0] = table[0, FLAG]
    ra_arrived()
    rb_arrived()
    wait_bytes(fac_a, loc.at[7])
    for swap, share, keep in (moves_a, moves_b):
        swap.wait_send()
        share.wait()
        keep.wait()
    wait_bytes(idbuf.at[pl.ds(0, NDP - 1)], ids_sem.at[0])
    for i in range(4):
        wait_bytes(owns[i][1].at[pl.ds(0, OWNED)], sib.at[0, i])
    for i in range(2):
        wait_bytes(parts.at[i, pl.ds(0, NT - 1)], psum_sem.at[i, 0])
        wait_bytes(sums.at[i, pl.ds(0, NT - 1)], psum_sem.at[i, 2])
    fa_finish()
    fb_finish()
    ra_finish()
    rb_finish()


def last_kernel(lists, fin_a, fin_b, fac, back, gh, ga, gb, acc_a, acc_b, buf_a, buf_b, ghb, gab, gbb, sems):
    count = lists[2, 0]

    def arriving(p):
        return (
            pltpu.make_async_copy(fin_a.at[lists[0, p] >> 5], buf_a.at[p], sems.at[0]),
            pltpu.make_async_copy(fin_b.at[lists[1, p] >> 5], buf_b.at[p], sems.at[4]),
        )

    def loop(step):
        def run(p, carry):
            step(p)
            return carry

        lax.fori_loop(0, count, run, 0)

    def start(p):
        for copy in arriving(p):
            copy.start()

    def wait(p):
        for copy in arriving(p):
            copy.wait()

    loop(start)
    for j in range(NBLK):
        rows = pl.ds(j * BLOCK, BLOCK)
        rows_out = adapter_scale * lax.dot_general(
            back[j], fac[j], (((0,), (0,)), ((), ())), preferred_element_type=jnp.float32
        )
        ghb[rows] = rows_out.astype(jnp.bfloat16)
        pltpu.make_async_copy(ghb.at[rows], gh.at[rows], sems.at[1]).start()
    gab[...] = jnp.zeros_like(gab)
    gbb[...] = jnp.zeros_like(gbb)
    trio = ((acc_a, buf_a, gab), (acc_b, buf_b, gbb))

    def clear(p):
        for acc, _, _ in trio:
            acc[lists[0, p] & 31] = jnp.zeros(acc.shape[1:], jnp.float32)

    def add(p):
        for acc, buf, _ in trio:
            acc[lists[0, p] & 31] += buf[p].astype(jnp.float32)

    def store(p):
        for acc, _, out in trio:
            out[lists[0, p] & 31] = acc[lists[0, p] & 31].astype(jnp.bfloat16)

    loop(clear)
    loop(wait)
    loop(add)
    loop(store)
    ca = pltpu.make_async_copy(gab, ga, sems.at[2])
    cb = pltpu.make_async_copy(gbb, gb, sems.at[3])
    ca.start()
    cb.start()
    pltpu.make_async_copy(ghb, gh, sems.at[1]).wait()
    ca.wait()
    cb.wait()


def shards(hidden, output_gradient, block_adapter_index, adapter_down_factors, adapter_up_factors):
    rows, ff_local = hidden.shape
    d_local = output_gradient.shape[1]
    hw, dw = ff_local // 2, d_local // 2
    bf16, f32 = jnp.bfloat16, jnp.float32
    vmem = pl.BlockSpec(memory_space=pltpu.VMEM)
    smem = pl.BlockSpec(memory_space=pltpu.SMEM)
    anywhere = pl.BlockSpec(memory_space=pl.ANY)
    dma = pltpu.SemaphoreType.DMA
    rank = ADAPTER_RANK
    streams = [
        pltpu.VMEM((2, slots, rank, width), bf16)
        for slots, width in ((SLOTS_OUT, hw), (EXPRESS, dw), (SLOTS_BACK, hw), (EXPRESS, dw))
    ]
    scratch = [
        pltpu.VMEM((NDP, 8, 128), jnp.int32),
        pltpu.VMEM((40, 128), jnp.int32),
        pltpu.SMEM((40, 128), jnp.int32),
        pltpu.VMEM((NBLK, rank, ff_local), bf16),
        pltpu.VMEM((NBLK, rank, d_local), bf16),
        pltpu.VMEM((NBLK, rank, BLOCK), bf16),
        pltpu.VMEM((rows, ff_local), bf16),
        pltpu.VMEM((rows, d_local), bf16),
        pltpu.VMEM((NBLK, rank, ff_local), bf16),
        pltpu.VMEM((NBLK, rank, d_local), bf16),
        pltpu.VMEM((2 * OWNED, rank, hw), bf16),
        pltpu.VMEM((2 * OWNED, rank, dw), bf16),
        pltpu.VMEM((2 * OWNED, rank, hw), bf16),
        pltpu.VMEM((2 * OWNED, rank, dw), bf16),
        pltpu.VMEM((2 * SLOTS_OUT, rank, hw), bf16),
        pltpu.VMEM((2 * EXPRESS, rank, dw), bf16),
        pltpu.VMEM((2 * NBLK, rank, hw), bf16),
        pltpu.VMEM((2 * NBLK, rank, dw), bf16),
        *streams,
        *streams,
        pltpu.VMEM((2 * SLOTS_OUT, rank, hw), bf16),
        pltpu.VMEM((2 * EXPRESS, rank, dw), bf16),
        pltpu.VMEM((2 * SLOTS_BACK, rank, hw), bf16),
        pltpu.VMEM((2 * EXPRESS, rank, dw), bf16),
        pltpu.VMEM((2, NT, 8, BLOCK), f32),
        pltpu.VMEM((2, NT, 8, BLOCK), f32),
        pltpu.VMEM((2, NT, 8, BLOCK), f32),
        dma((8,)),
        dma((2,)),
        dma((2, 4)),
        dma((2, 5)),
        dma((4,)),
        dma((4, 2, max(SLOTS_OUT, SLOTS_BACK))),
        dma((4, 3)),
        dma((2, 4)),
    ]
    flag, lists, fac, back, fin_a, fin_b = pl.pallas_call(
        functools.partial(ring_kernel, hw, dw),
        name="ring",
        out_shape=(
            jax.ShapeDtypeStruct((1,), jnp.int32),
            jax.ShapeDtypeStruct((8, 128), jnp.int32),
            jax.ShapeDtypeStruct((NBLK, rank, ff_local), bf16),
            jax.ShapeDtypeStruct((NBLK, rank, BLOCK), bf16),
            jax.ShapeDtypeStruct((NFIN, rank, ff_local), bf16),
            jax.ShapeDtypeStruct((NFIN, rank, d_local), bf16),
        ),
        in_specs=[smem] + [anywhere] * 4,
        out_specs=(smem, vmem, anywhere, vmem, anywhere, anywhere),
        scratch_shapes=scratch,
        compiler_params=pltpu.CompilerParams(
            collective_id=0, has_side_effects=True, vmem_limit_bytes=VMEM_LIMIT
        ),
    )(block_adapter_index, hidden, output_gradient, adapter_down_factors, adapter_up_factors)

    def finish(*_):
        return pl.pallas_call(
            last_kernel,
            name="finish",
            out_shape=(
                jax.ShapeDtypeStruct((rows, ff_local), bf16),
                jax.ShapeDtypeStruct(adapter_down_factors.shape, bf16),
                jax.ShapeDtypeStruct(adapter_up_factors.shape, bf16),
            ),
            in_specs=[smem, anywhere, anywhere, vmem, vmem],
            out_specs=(anywhere, anywhere, anywhere),
            scratch_shapes=[
                pltpu.VMEM((OWNED, rank, ff_local), f32),
                pltpu.VMEM((OWNED, rank, d_local), f32),
                pltpu.VMEM((NFIN, rank, ff_local), bf16),
                pltpu.VMEM((NFIN, rank, d_local), bf16),
                pltpu.VMEM((rows, ff_local), bf16),
                pltpu.VMEM((OWNED, rank, ff_local), bf16),
                pltpu.VMEM((OWNED, rank, d_local), bf16),
                dma((5,)),
            ],
            compiler_params=pltpu.CompilerParams(vmem_limit_bytes=VMEM_LIMIT),
        )(lists, fin_a, fin_b, fac, back)

    return lax.cond(
        flag[0] > 0,
        finish,
        general,
        hidden,
        output_gradient,
        block_adapter_index,
        adapter_down_factors,
        adapter_up_factors,
    )


def solution(mesh):
    placed = (
        P("dp", "tensor"),
        P("dp", "tensor"),
        P("dp"),
        P("dp", None, "tensor"),
        P("dp", None, "tensor"),
    )
    return jax.shard_map(
        shards,
        mesh=mesh,
        in_specs=placed,
        out_specs=(P("dp", "tensor"), P("dp", None, "tensor"), P("dp", None, "tensor")),
        check_vma=False,
    )
```
